128 devices in a mesh: row: 8 (over y, z_hi), col: 16 (over z_lo, x, core).
Axes of the slice: x: 4, y: 4, z: 4 (z_hi: 2, z_lo: 2; z = z_hi * 2 + z_lo), core: 2. Of those that a mesh axis runs over, the one named last changes fastest.
Arguments:
- base: bfloat16 [2, 8192, 29568], P(None, ('row', 'col')), may hold values from -21 to 21
- adjusted: bfloat16 [2, 8192, 29568], P(None, ('row', 'col')), may hold values from -21 to 21
- omega: bfloat16 [29568, 512], P('col'), may hold values from -0.03125 to 0.03125
Outputs:
- basis: float32 [2, 8192, 512], P(None, ('row', 'col'))
- projected: float32 [2, 512, 29568], P(None, 'row', 'col')
The draws below stay inside these ranges and needn't reach their ends.
All inputs are finite; a program needn't handle non-finite values.
Results may differ from the reference program's by a relative error of at most 0.005.
Values may be sent and summed in bfloat16 or wider, within the bound.
A program may use at most 128 MiB of HBM per device.

```python
import math
import jax
import jax.numpy as jnp
from jax import lax

D = 8192
FF = 29568
R = 512
MATS = 2


def weight_field(key, spread):
    key_factor, key_value = jax.random.split(key)
    rising = 3.0 ** (jnp.arange(D, dtype=jnp.float32) / (D - 1))
    factor = jnp.exp(jax.random.uniform(key_factor, (MATS, D, 1), jnp.float32) * math.log(spread))
    values = jnp.clip(jax.random.normal(key_value, (MATS, D, FF), jnp.float32), -5.0, 5.0)
    scaled = values * rising[None, :, None] * factor * 0.5
    return scaled.astype(jnp.bfloat16)


def draw_base(key, part):
    key = jax.random.fold_in(key, 11)
    return weight_field(key, 2.0)


def draw_adjusted(key, part):
    key = jax.random.fold_in(key, 23)
    return weight_field(key, 2.0)


def steps_of(key, shape, cuts, least, largest):
    loudness, own = 1.0, jax.random.fold_in(key, 6)
    for axis_at, shards_of in cuts:
        draws = jnp.exp(jax.random.uniform(jax.random.fold_in(own, axis_at), (shards_of,), jnp.float32, least / len(cuts), largest / len(cuts)))
        loudness = loudness * jnp.repeat(draws, shape[axis_at] // shards_of).reshape([-1 if axis == axis_at else 1 for axis in range(len(shape))])
    return loudness


def centred(own_key, dims, scale, most, cuts=(), held_as=jnp.bfloat16):
    result = scale * jax.random.normal(own_key, dims, jnp.float32)
    if cuts:
        result = result * steps_of(own_key, dims, cuts, -0.22, 0.18)
    return jnp.clip(result, -most, most).astype(held_as)


def setup_inputs(seed: int = 0) -> dict:
    key_of = jax.random.split(jax.random.key(seed), 4)
    base = draw_base(jax.random.fold_in(key_of[3], 71), 0)
    adjusted = draw_adjusted(jax.random.fold_in(key_of[3], 71), 0)
    omega = centred(key_of[2], (FF, R), FF ** -0.5, 0.03125, ((0, 16),))
    return dict(base=base, adjusted=adjusted, omega=omega)


def reference(base, adjusted, omega):
    basis_list = []
    proj_list = []
    for m in range(MATS):
        delta = (adjusted[m].astype(jnp.float32) - base[m].astype(jnp.float32)).astype(jnp.bfloat16)
        sketch = jnp.dot(delta.astype(jnp.float32), omega.astype(jnp.float32), preferred_element_type=jnp.float32)
        gram = jnp.dot(sketch.T, sketch, precision=lax.Precision.HIGHEST) / D
        lower = jnp.linalg.cholesky(gram)
        basis = lax.linalg.triangular_solve(lower, sketch, left_side=False, lower=True, transpose_a=True)
        basis_low = basis.astype(jnp.bfloat16)
        proj = jnp.dot(basis_low.T.astype(jnp.float32), delta.astype(jnp.float32), preferred_element_type=jnp.float32) / math.sqrt(D)
        basis_list.append(basis)
        proj_list.append(proj)
    return (jnp.stack(basis_list), jnp.stack(proj_list))
```

```python
import math

import jax
import jax.numpy as jnp
from jax import lax
from jax.experimental import pallas as pl
from jax.experimental.pallas import tpu as pltpu
from jax.sharding import PartitionSpec as P

MESH = pl.DeviceIdType.MESH
HIGH = lax.Precision.HIGHEST
D = 8192
FF = 29568
R = 512
MATS = 2
ROWS = 64
BLOCK = 1848
WIDE = 1920
WINDOW = 2048
STAGES = 4
COLS = 16
TILE = 128
HEIGHTS = (32, 24, 16, 8)
STARTS = (0, 32, 56, 72)
SLAB = 80


def f32(x):
    return x.astype(jnp.float32)


def dot_nt(a, b, precision=None):
    return lax.dot_general(
        a, b, (((1,), (1,)), ((), ())), precision=precision, preferred_element_type=jnp.float32
    )


def dot_tn(a, b, precision=None):
    return lax.dot_general(
        a, b, (((0,), (0,)), ((), ())), precision=precision, preferred_element_type=jnp.float32
    )


def dot_nn(a, b, precision=None):
    return jnp.dot(a, b, precision=precision, preferred_element_type=jnp.float32)


def invert_factor(block):
    count = TILE // 8
    rows = [block[8 * i : 8 * i + 8, :] for i in range(count)]
    shape = (8, TILE)
    lane = lax.broadcasted_iota(jnp.int32, shape, 1)
    sub = lax.broadcasted_iota(jnp.int32, shape, 0)
    for s in range(count):
        cols = {
            (i, j): jnp.broadcast_to(rows[i][:, 8 * s + j : 8 * s + j + 1], shape)
            for i in range(s, count)
            for j in range(8)
        }
        for j in range(8):
            here = lane == 8 * s + j
            pivot = jnp.broadcast_to(cols[s, j][j : j + 1, :], shape)
            inverse = 1.0 / pivot
            row = jnp.where(here, 1.0, jnp.broadcast_to(rows[s][j : j + 1, :], shape))
            heads = {
                j2: jnp.broadcast_to(cols[s, j2][j : j + 1, :], shape) for j2 in range(j + 1, 8)
            }
            for i in range(s, count):
                factor = cols[i, j] * inverse
                clear = here
                if i == s:
                    factor = jnp.where(sub > j, factor, 0.0)
                    clear = here & (sub > j)
                rows[i] = jnp.where(clear, 0.0, rows[i]) - factor * row
                for j2 in range(j + 1, 8):
                    cols[i, j2] = cols[i, j2] - factor * heads[j2]
    out = []
    for i in range(count):
        at = sub + 8 * i
        diagonal = jnp.sum(jnp.where(lane == at, rows[i], 0.0), axis=1, keepdims=True)
        unit = jnp.where(lane < at, rows[i], jnp.where(lane == at, 1.0, 0.0))
        out.append(unit * (1.0 / jnp.sqrt(diagonal)))
    return jnp.concatenate(out, axis=0)


def kernel(
    base_ref, adjusted_ref, omega_ref, basis_ref, projected_ref,
    old, new, source, held, omega_pad, keep, odd, pre, part, rows_all,
    gram, packed, slabs, total, across, spread, low, inv, basis_t, out_part, in_part,
    load_sem, send_sem, recv_sem, odd_send, odd_recv, part_send, part_recv,
    rows_send, rows_recv, core_send, core_recv, slab_send, slab_recv, x_send, x_recv,
    spread_send, spread_recv, inv_send, inv_recv, out_send, out_recv,
):
    r, c = lax.axis_index("row"), lax.axis_index("col")
    y, z_hi = r // 2, r % 2
    z_lo, x, k = c // 8, (c // 2) % 4, c % 2
    z = z_hi * 2 + z_lo
    q = y * 4 + z

    def col_of(z_lo_, x_, k_):
        return z_lo_ * 8 + x_ * 2 + k_

    def partner_col(i, sign):
        dx, dz, dk = i // 4, (i // 2) % 2, i % 2
        return col_of((z_lo + dz) % 2, (x + sign * dx + 4) % 4, (k + dk) % 2)

    def plane(q_):
        y_, z_ = q_ // 4, q_ % 4
        return (y_ * 2 + z_ // 2, col_of(z_ % 2, x, k))

    def xor(a, d, bits):
        out = 0
        for bit in range(bits):
            own = (a // (1 << bit)) % 2
            out = out + ((own + (d // (1 << bit)) % 2) % 2) * (1 << bit)
        return out

    twin = (r, col_of(z_lo, x, 1 - k))

    def window(f):
        first = (BLOCK * f) // TILE
        start = jnp.minimum(first, (FF - WINDOW) // TILE)
        return start, first - start, BLOCK * f - first * TILE

    def loads(i):
        start, _, _ = window(partner_col(i, 1))
        span = pl.ds(pl.multiple_of(start * TILE, TILE), WINDOW)
        slot = i % STAGES
        return [
            pltpu.make_async_copy(
                src.at[:, :, span], dst.at[slot, :, :, pl.ds(0, WINDOW)], load_sem.at[n, slot]
            )
            for n, (src, dst) in enumerate(((base_ref, old), (adjusted_ref, new)))
        ]

    for i in range(STAGES):
        for copy in loads(i):
            copy.start()

    barrier = pltpu.get_barrier_semaphore()
    for i in range(1, COLS):
        pl.semaphore_signal(
            barrier, inc=1, device_id=(r, partner_col(i, 1)), device_id_type=MESH
        )
    for d in range(1, COLS):
        pl.semaphore_signal(barrier, inc=1, device_id=plane(xor(q, d, 4)), device_id_type=MESH)

    omega_pad[0:1840, :] = omega_ref[0:1840, :]
    tail = f32(omega_ref[1840:1848, :])
    omega_pad[1840:1856, :] = jnp.concatenate([tail, jnp.zeros_like(tail)], axis=0).astype(
        jnp.bfloat16
    )
    omega_pad[1856:1920, :] = jnp.zeros((64, R), jnp.bfloat16)

    lane = lax.broadcasted_iota(jnp.int32, (ROWS, TILE), 1)

    def shifted(i, put):
        _, skip, ahead = window(partner_col(i, 1))
        slot = i % STAGES
        turn = (TILE - ahead) % TILE
        for m in range(MATS):
            last = None
            for t in range(16):
                span = pl.ds(pl.multiple_of((t + skip) * TILE, TILE), TILE)
                tile = f32(new[slot, m, :, span]) - f32(old[slot, m, :, span])
                tile = pltpu.roll(tile, turn, 1)
                if t > 0:
                    value = jnp.where(lane < TILE - ahead, last, tile)
                    if t == 15:
                        value = jnp.where(lane < BLOCK - 14 * TILE, value, 0.0)
                    put(m, (t - 1) * TILE, value.astype(jnp.bfloat16))
                last = tile

    def put_own(m, at, value):
        held[m, 0, :, at : at + TILE] = value

    for copy in loads(0):
        copy.wait()
    shifted(0, put_own)
    for copy in loads(STAGES):
        copy.start()
    pl.semaphore_wait(barrier, 2 * (COLS - 1))

    def delta_copy(m, i):
        return pltpu.make_async_remote_copy(
            src_ref=source.at[m, i],
            dst_ref=held.at[m, i],
            send_sem=send_sem.at[m, i],
            recv_sem=recv_sem.at[m, i],
            device_id=(r, partner_col(i, 1)),
            device_id_type=MESH,
        )

    def send_step(i, carry):
        for copy in loads(i):
            copy.wait()

        def put(m, at, value):
            source[m, i, :, at : at + TILE] = value

        shifted(i, put)

        @pl.when(i + STAGES < COLS)
        def _():
            for copy in loads(i + STAGES):
                copy.start()

        for m in range(MATS):
            delta_copy(m, i).start()
        return carry

    lax.fori_loop(1, COLS, send_step, 0)

    def odd_copy(m, g):
        return pltpu.make_async_remote_copy(
            src_ref=odd.at[m, g],
            dst_ref=pre.at[m, g],
            send_sem=odd_send.at[m, g],
            recv_sem=odd_recv.at[m, g],
            device_id=twin,
            device_id_type=MESH,
        )

    def part_copy(m, e):
        dx, dz = e // 2, e % 2
        to = (r, col_of((z_lo + dz) % 2, (x - dx + 4) % 4, k))
        return pltpu.make_async_remote_copy(
            src_ref=keep.at[m, e],
            dst_ref=part.at[m, e],
            send_sem=part_send.at[m, e],
            recv_sem=part_recv.at[m, e],
            device_id=to,
            device_id_type=MESH,
        )

    def sketch(m, g):
        block = held[m, pl.ds(4 * g, 4)].reshape(4 * ROWS, WIDE)
        got = dot_nn(block, omega_pad[...]).reshape(4, ROWS, R)
        keep[m, 2 * g] = got[0]
        odd[m, g, 0] = got[1]
        keep[m, 2 * g + 1] = got[2]
        odd[m, g, 1] = got[3]
        odd_copy(m, g).start()

    def hand_on(m, g):
        odd_copy(m, g).wait_recv()
        for h in range(2):
            keep[m, 2 * g + h] = keep[m, 2 * g + h] + pre[m, g, h]

    for m in range(MATS):
        for i in range(1, 4):
            delta_copy(m, i).wait_recv()
        sketch(m, 0)

    def sketch_step(g, carry):
        for m in range(MATS):
            for i in range(4):
                delta_copy(m, 4 * g + i).wait_recv()
            sketch(m, g)
        for m in range(MATS):
            hand_on(m, g - 1)
            for h in range(2):
                @pl.when(2 * (g - 1) + h > 0)
                def _():
                    part_copy(m, 2 * (g - 1) + h).start()
        return carry

    lax.fori_loop(1, 4, sketch_step, 0)
    for m in range(MATS):
        hand_on(m, 3)
        for h in range(2):
            part_copy(m, 6 + h).start()

    for m in range(MATS):
        value = keep[m, 0]
        for e in range(1, 8):
            part_copy(m, e).wait_recv()
            value = value + part[m, e]
        rows_all[0, m] = value

    def rows_core(e):
        return pltpu.make_async_remote_copy(
            src_ref=rows_all.at[2 * e],
            dst_ref=rows_all.at[2 * e + 1],
            send_sem=core_send.at[e],
            recv_sem=core_recv.at[e],
            device_id=twin,
            device_id_type=MESH,
        )

    def rows_copy(e):
        dx, dz = e // 2, e % 2
        to = (r, col_of((z_lo + dz) % 2, (x + dx) % 4, k))
        return pltpu.make_async_remote_copy(
            src_ref=rows_all.at[0],
            dst_ref=rows_all.at[2 * e],
            send_sem=rows_send.at[e],
            recv_sem=rows_recv.at[e],
            device_id=to,
            device_id_type=MESH,
        )

    rows_core(0).start()
    for e in range(1, 8):
        rows_copy(e).start()

    rows_core(0).wait_recv()
    mine = jnp.concatenate([rows_all[0, k], rows_all[1, k]], axis=0)
    gram[...] = dot_tn(mine, mine, HIGH) * (1.0 / D)
    for p in range(16):
        for j in range(4):
            h, at = HEIGHTS[j], STARTS[j]
            top = TILE * j + p * h
            packed[p, at : at + h, :] = gram[top : top + h, TILE * j : TILE * j + TILE]

    def slab_copy(d):
        to = xor(q, d, 4)
        return pltpu.make_async_remote_copy(
            src_ref=packed.at[to],
            dst_ref=slabs.at[d],
            send_sem=slab_send.at[d],
            recv_sem=slab_recv.at[d],
            device_id=plane(to),
            device_id_type=MESH,
        )

    for d in range(1, 16):
        slab_copy(d).start()
    value = packed[q]
    for d in range(1, 16):
        slab_copy(d).wait_recv()
        value = value + slabs[d]
    total[...] = value

    def x_copy(d):
        return pltpu.make_async_remote_copy(
            src_ref=total,
            dst_ref=across.at[d],
            send_sem=x_send.at[d],
            recv_sem=x_recv.at[d],
            device_id=(r, col_of(z_lo, xor(x, d, 2), k)),
            device_id_type=MESH,
        )

    for d in range(1, 4):
        x_copy(d).start()
    for d in range(1, 4):
        x_copy(d).wait_recv()
    spread[q] = (total[...] + across[1]) + (across[2] + across[3])

    def spread_copy(d):
        return pltpu.make_async_remote_copy(
            src_ref=spread.at[q],
            dst_ref=spread.at[q],
            send_sem=spread_send.at[d],
            recv_sem=spread_recv.at[d],
            device_id=plane(xor(q, d, 4)),
            device_id_type=MESH,
        )

    def spread_arrival(d):
        other = xor(q, d, 4)
        return pltpu.make_async_remote_copy(
            src_ref=spread.at[other],
            dst_ref=spread.at[other],
            send_sem=spread_send.at[d],
            recv_sem=spread_recv.at[d],
            device_id=plane(other),
            device_id_type=MESH,
        )

    for d in range(1, 16):
        spread_copy(d).start()
    for e in range(1, 8):
        rows_copy(e).wait_recv()
        rows_core(e).start()
    for d in range(1, 16):
        spread_arrival(d).wait_recv()

    gram[...] = jnp.zeros((R, R), jnp.float32)
    for p in range(16):
        for j in range(4):
            h, at = HEIGHTS[j], STARTS[j]
            top = TILE * j + p * h
            gram[top : top + h, TILE * j : TILE * j + TILE] = spread[p, at : at + h, :]

    low[...] = jnp.zeros((R, R), jnp.float32)
    inv[k] = jnp.zeros((R, R), jnp.float32)
    row_at = lax.broadcasted_iota(jnp.int32, (R, TILE), 0)

    def factor_step(b, carry):
        span = pl.ds(pl.multiple_of(b * TILE, TILE), TILE)
        own = invert_factor(gram[span, span])
        panel = dot_nt(gram[:, span], own, HIGH)
        panel = jnp.where(row_at >= (b + 1) * TILE, panel, 0.0)
        done = dot_nn(low[span, :], inv[k], HIGH)
        inv[k, span, :] = -dot_nn(own, done, HIGH)
        inv[k, span, span] = own
        low[:, span] = panel
        gram[...] = gram[...] - dot_nt(panel, panel, HIGH)
        return carry

    lax.fori_loop(0, R // TILE, factor_step, 0)

    inv_copy = pltpu.make_async_remote_copy(
        src_ref=inv.at[k],
        dst_ref=inv.at[k],
        send_sem=inv_send,
        recv_sem=inv_recv,
        device_id=twin,
        device_id_type=MESH,
    )
    inv_arrival = pltpu.make_async_remote_copy(
        src_ref=inv.at[1 - k],
        dst_ref=inv.at[1 - k],
        send_sem=inv_send,
        recv_sem=inv_recv,
        device_id=twin,
        device_id_type=MESH,
    )
    inv_copy.start()
    for e in range(1, 8):
        rows_core(e).wait_recv()
    inv_arrival.wait_recv()

    def out_copy(m, d):
        to = xor(r, d, 3)
        return pltpu.make_async_remote_copy(
            src_ref=out_part.at[m, to],
            dst_ref=in_part.at[m, d],
            send_sem=out_send.at[m, d],
            recv_sem=out_recv.at[m, d],
            device_id=(to, c),
            device_id_type=MESH,
        )

    for m in range(MATS):
        basis_t[...] = dot_nt(inv[m], rows_all[:, m].reshape(COLS * ROWS, R), HIGH).astype(
            jnp.bfloat16
        )

        def project_step(n, carry):
            span = pl.ds(pl.multiple_of(n * 384, TILE), 384)
            block = held[m, :, :, span].reshape(COLS * ROWS, 384)
            got = dot_nn(basis_t[...], block)
            out_part[m, :, :, span] = got.reshape(8, ROWS, 384).astype(jnp.bfloat16)
            return carry

        lax.fori_loop(0, WIDE // 384, project_step, 0)
        for d in range(1, 8):
            out_copy(m, d).start()

    for m in range(MATS):
        basis_ref[m] = dot_nt(rows_all[0, m], inv[m], HIGH)

    for m in range(MATS):
        for d in range(1, 8):
            out_copy(m, d).wait_recv()
        value = f32(out_part[m, r])
        for d in range(1, 8):
            value = value + f32(in_part[m, d])
        projected_ref[m] = value[:, :BLOCK] * (1.0 / math.sqrt(D))

    for m in range(MATS):
        for i in range(1, COLS):
            delta_copy(m, i).wait_send()
        for g in range(4):
            odd_copy(m, g).wait_send()
        for e in range(1, 8):
            part_copy(m, e).wait_send()
        for d in range(1, 8):
            out_copy(m, d).wait_send()
    for e in range(8):
        rows_core(e).wait_send()
    for e in range(1, 8):
        rows_copy(e).wait_send()
    for d in range(1, 16):
        slab_copy(d).wait_send()
        spread_copy(d).wait_send()
    for d in range(1, 4):
        x_copy(d).wait_send()
    inv_copy.wait_send()


def body(base, adjusted, omega):
    f, b16, sem = jnp.float32, jnp.bfloat16, pltpu.SemaphoreType.DMA
    any_space, vmem = pl.BlockSpec(memory_space=pl.ANY), pl.BlockSpec(memory_space=pltpu.VMEM)
    scratch = [
        pltpu.VMEM((STAGES, MATS, ROWS, WINDOW + TILE), b16),
        pltpu.VMEM((STAGES, MATS, ROWS, WINDOW + TILE), b16),
        pltpu.VMEM((MATS, COLS, ROWS, WIDE), b16),
        pltpu.VMEM((MATS, COLS, ROWS, WIDE), b16),
        pltpu.VMEM((WIDE, R), b16),
        pltpu.VMEM((MATS, 8, ROWS, R), f),
        pltpu.VMEM((MATS, 4, 2, ROWS, R), f),
        pltpu.VMEM((MATS, 4, 2, ROWS, R), f),
        pltpu.VMEM((MATS, 8, ROWS, R), f),
        pltpu.VMEM((COLS, MATS, ROWS, R), f),
        pltpu.VMEM((R, R), f),
        pltpu.VMEM((16, SLAB, TILE), f),
        pltpu.VMEM((16, SLAB, TILE), f),
        pltpu.VMEM((SLAB, TILE), f),
        pltpu.VMEM((4, SLAB, TILE), f),
        pltpu.VMEM((16, SLAB, TILE), f),
        pltpu.VMEM((R, R), f),
        pltpu.VMEM((MATS, R, R), f),
        pltpu.VMEM((R, COLS * ROWS), b16),
        pltpu.VMEM((MATS, 8, ROWS, WIDE), b16),
        pltpu.VMEM((MATS, 8, ROWS, WIDE), b16),
        sem((2, STAGES)),
        sem((MATS, COLS)), sem((MATS, COLS)),
        sem((MATS, 4)), sem((MATS, 4)),
        sem((MATS, 8)), sem((MATS, 8)),
        sem((8,)), sem((8,)),
        sem((8,)), sem((8,)),
        sem((16,)), sem((16,)),
        sem((4,)), sem((4,)),
        sem((16,)), sem((16,)),
        sem, sem,
        sem((MATS, 8)), sem((MATS, 8)),
    ]
    return pl.pallas_call(
        kernel,
        out_shape=(
            jax.ShapeDtypeStruct((MATS, ROWS, R), f),
            jax.ShapeDtypeStruct((MATS, ROWS, BLOCK), f),
        ),
        in_specs=[any_space, any_space, vmem],
        out_specs=(vmem, vmem),
        scratch_shapes=scratch,
        compiler_params=pltpu.CompilerParams(
            collective_id=0, has_side_effects=True, vmem_limit_bytes=62 << 20
        ),
        cost_estimate=pl.CostEstimate(
            flops=10_000_000_000, bytes_accessed=20_000_000, transcendentals=0
        ),
        name="sketch_project",
    )(base, adjusted, omega)


def solution(mesh):
    placed = (P(None, ("row", "col"), None), P(None, ("row", "col"), None), P("col", None))
    return jax.shard_map(
        body,
        mesh=mesh,
        in_specs=placed,
        out_specs=(P(None, ("row", "col"), None), P(None, "row", "col")),
        check_vma=False,
    )
```

```python
import math

import jax
import jax.numpy as jnp
from jax import lax
from jax.experimental import pallas as pl
from jax.experimental.pallas import tpu as pltpu
from jax.sharding import PartitionSpec as P

MESH = pl.DeviceIdType.MESH
HIGH = lax.Precision.HIGHEST
D = 8192
FF = 29568
R = 512
MATS = 2
ROWS = 64
BLOCK = 1848
WIDE = 1920
WINDOW = 2048
STAGES = 4
COLS = 16
TILE = 128
HEIGHTS = (32, 24, 16, 8)
STARTS = (0, 32, 56, 72)
SLAB = 80


def f32(x):
    return x.astype(jnp.float32)


def dot_nt(a, b, precision=None):
    return lax.dot_general(
        a, b, (((1,), (1,)), ((), ())), precision=precision, preferred_element_type=jnp.float32
    )


def dot_tn(a, b, precision=None):
    return lax.dot_general(
        a, b, (((0,), (0,)), ((), ())), precision=precision, preferred_element_type=jnp.float32
    )


def dot_nn(a, b, precision=None):
    return jnp.dot(a, b, precision=precision, preferred_element_type=jnp.float32)


def invert_factor(block):
    count = TILE // 8
    rows = [block[8 * i : 8 * i + 8, :] for i in range(count)]
    shape = (8, TILE)
    lane = lax.broadcasted_iota(jnp.int32, shape, 1)
    sub = lax.broadcasted_iota(jnp.int32, shape, 0)
    for s in range(count):
        cols = {
            (i, j): jnp.broadcast_to(rows[i][:, 8 * s + j : 8 * s + j + 1], shape)
            for i in range(s, count)
            for j in range(8)
        }
        for j in range(8):
            here = lane == 8 * s + j
            pivot = jnp.broadcast_to(cols[s, j][j : j + 1, :], shape)
            inverse = 1.0 / pivot
            row = jnp.where(here, 1.0, jnp.broadcast_to(rows[s][j : j + 1, :], shape))
            heads = {
                j2: jnp.broadcast_to(cols[s, j2][j : j + 1, :], shape) for j2 in range(j + 1, 8)
            }
            for i in range(s, count):
                factor = cols[i, j] * inverse
                clear = here
                if i == s:
                    factor = jnp.where(sub > j, factor, 0.0)
                    clear = here & (sub > j)
                rows[i] = jnp.where(clear, 0.0, rows[i]) - factor * row
                for j2 in range(j + 1, 8):
                    cols[i, j2] = cols[i, j2] - factor * heads[j2]
    out = []
    for i in range(count):
        at = sub + 8 * i
        diagonal = jnp.sum(jnp.where(lane == at, rows[i], 0.0), axis=1, keepdims=True)
        unit = jnp.where(lane < at, rows[i], jnp.where(lane == at, 1.0, 0.0))
        out.append(unit * (1.0 / jnp.sqrt(diagonal)))
    return jnp.concatenate(out, axis=0)


def kernel(
    base_ref, adjusted_ref, omega_ref, basis_ref, projected_ref,
    old, new, source, held, omega_pad, keep, odd, pre, part, rows_all,
    gram, packed, slabs, total, across, spread, low, inv, basis_t, out_part, in_part,
    load_sem, omega_send, omega_recv, own_sem, send_sem, recv_sem, odd_send, odd_recv, part_send, part_recv,
    rows_send, rows_recv, core_send, core_recv, slab_send, slab_recv, x_send, x_recv,
    spread_send, spread_recv, inv_send, inv_recv, out_send, out_recv, own_out_sem,
):
    r, c = lax.axis_index("row"), lax.axis_index("col")
    y, z_hi = r // 2, r % 2
    z_lo, x, k = c // 8, (c // 2) % 4, c % 2
    z = z_hi * 2 + z_lo
    q = y * 4 + z

    def col_of(z_lo_, x_, k_):
        return z_lo_ * 8 + x_ * 2 + k_

    def offsets(s):
        t, g, u, near = s % 3, s // 3, (s + 4) % 16, s // 12
        dx = (1 + 2 * t - 3 * (t // 2)) * (1 - near)
        dz = ((g + 1) % 2) * (1 - near) + ((u + 1) % 2) * near
        dk = (g // 2) * (1 - near) + (((u + 1) // 2) % 2) * near
        return dx, dz, dk

    def place(m, s, sign):
        dx, dz, dk = offsets(s)
        y_ = (y + m * sign * dx + 4) % 4
        x_ = (x + (1 - m) * sign * dx + 4) % 4
        z_ = (z + dz * (2 * z_lo - 1) * (2 * m - 1) + 4) % 4
        return x_, y_, z_, (k + dk) % 2

    def device(x_, y_, z_, k_):
        return (y_ * 2 + z_ // 2, col_of(z_ % 2, x_, k_))

    def member(m, s, sign=1):
        return device(*place(m, s, sign))

    def turned(x_, y_, k_):
        return (x_ + y_ * (1 - 2 * k_) + 4) % 4

    def block_of(m, s):
        x_, y_, z_, k_ = place(m, s, 1)
        return col_of(z_ % 2, (1 - m) * x_ + m * turned(x_, y_, k_), k_)

    mine_steps = (0, 1, 2, 3, 4, 5, 12, 15)
    twin_steps = (6, 7, 8, 9, 10, 11, 14, 13)

    def plane(q_):
        y_, z_ = q_ // 4, q_ % 4
        return (y_ * 2 + z_ // 2, col_of(z_ % 2, x, k))

    def xor(a, d, bits):
        out = 0
        for bit in range(bits):
            own = (a // (1 << bit)) % 2
            out = out + ((own + (d // (1 << bit)) % 2) % 2) * (1 << bit)
        return out

    twin = (r, col_of(z_lo, x, 1 - k))
    pending = []

    def finish():
        for copy in pending:
            copy.wait_send()

        @pl.when(omega_sends > 0)
        def _():
            omega_copy(omega_to).wait_send()

    def window(f):
        first = (BLOCK * f) // TILE
        start = jnp.minimum(first, (FF - WINDOW) // TILE)
        return start, first - start, BLOCK * f - first * TILE

    def loads(i):
        slot, out = i % STAGES, []
        for m in range(MATS):
            start, _, _ = window(block_of(m, i))
            span = pl.ds(pl.multiple_of(start * TILE, TILE), WINDOW)
            for n, (src, dst) in enumerate(((base_ref, old), (adjusted_ref, new))):
                out.append(
                    pltpu.make_async_copy(
                        src.at[m, :, span],
                        dst.at[slot, m, :, pl.ds(0, WINDOW)],
                        load_sem.at[n, m, slot],
                    )
                )
        return out

    for i in range(STAGES):
        for copy in loads(i):
            copy.start()

    barrier = pltpu.get_barrier_semaphore()
    def greet(to):
        pl.semaphore_signal(barrier, inc=1, device_id=to, device_id_type=MESH)

    for i in range(COLS - 1):
        for m in range(MATS):
            greet(member(m, i))
    for d in range(1, COLS):
        greet(plane(xor(q, d, 4)))

    def owner(to):
        return device(turned(x, y, k), to // 2, (to % 2) * 2 + z_lo, k)

    def holder(of):
        y_ = of // 2
        return device((x - y_ * (1 - 2 * k) + 4) % 4, y_, (of % 2) * 2 + z_lo, k)

    at_zero = 1 - (y + 3) // 4
    for d in range(8):
        to = xor(r, d, 3)
        if d == 0:
            @pl.when(y > 0)
            def _():
                greet(owner(to))
                greet(holder(to))
        else:
            greet(owner(to))
            greet(holder(to))

    omega_pad[0, 0:1840, :] = omega_ref[0:1840, :]
    tail = f32(omega_ref[1840:1848, :])
    omega_pad[0, 1840:1856, :] = jnp.concatenate([tail, jnp.zeros_like(tail)], axis=0).astype(
        jnp.bfloat16
    )
    omega_pad[0, 1856:1920, :] = jnp.zeros((64, R), jnp.bfloat16)

    lane = lax.broadcasted_iota(jnp.int32, (ROWS, TILE), 1)

    def shifted(i, put):
        slot = i % STAGES
        for m in range(MATS):
            _, skip, ahead = window(block_of(m, i))
            turn = (TILE - ahead) % TILE
            last = None
            for t in range(16):
                span = pl.ds(pl.multiple_of((t + skip) * TILE, TILE), TILE)
                tile = f32(new[slot, m, :, span]) - f32(old[slot, m, :, span])
                tile = pltpu.roll(tile, turn, 1)
                if t > 0:
                    value = jnp.where(lane < TILE - ahead, last, tile)
                    if t == 15:
                        value = jnp.where(lane < BLOCK - 14 * TILE, value, 0.0)
                    put(m, (t - 1) * TILE, value.astype(jnp.bfloat16))
                last = tile

    pl.semaphore_wait(barrier, 3 * (COLS - 1) + 16 - 2 * at_zero)

    def omega_copy(to):
        return pltpu.make_async_remote_copy(
            src_ref=omega_pad.at[0],
            dst_ref=omega_pad.at[1],
            send_sem=omega_send,
            recv_sem=omega_recv,
            device_id=to,
            device_id_type=MESH,
        )

    from_zero = (y // 2) * (1 - y % 2) * k
    to_two = at_zero * k
    omega_to = device((x - y * (1 - 2 * k) + 2 * to_two + 4) % 4, y + 2 * to_two, z, k)
    omega_sends = (1 - at_zero) * (1 - from_zero) + to_two
    own_omega = pltpu.make_async_copy(omega_pad.at[0], omega_pad.at[1], own_sem)

    @pl.when(omega_sends > 0)
    def _():
        omega_copy(omega_to).start()

    @pl.when(at_zero > 0)
    def _():
        own_omega.start()

    def delta_copy(m, i):
        return pltpu.make_async_remote_copy(
            src_ref=source.at[m, i],
            dst_ref=held.at[m, i],
            send_sem=send_sem.at[m, i],
            recv_sem=recv_sem.at[m, i],
            device_id=member(m, i),
            device_id_type=MESH,
        )

    def send_step(i, carry):
        for copy in loads(i):
            copy.wait()

        def put(m, at, value):
            source[m, i, :, at : at + TILE] = value

        shifted(i, put)

        @pl.when(i + STAGES < COLS)
        def _():
            for copy in loads(i + STAGES):
                copy.start()

        for m in range(MATS):
            delta_copy(m, i).start()
        return carry

    lax.fori_loop(0, COLS - 1, send_step, 0)
    pending += [delta_copy(m, i) for m in range(MATS) for i in range(COLS - 1)]

    def put_own(m, at, value):
        held[m, COLS - 1, :, at : at + TILE] = value

    for copy in loads(COLS - 1):
        copy.wait()
    shifted(COLS - 1, put_own)

    def odd_copy(m, g):
        span = pl.ds(6 * g, 6 - 4 * g)
        return pltpu.make_async_remote_copy(
            src_ref=odd.at[m, span],
            dst_ref=pre.at[m, span],
            send_sem=odd_send.at[m, g],
            recv_sem=odd_recv.at[m, g],
            device_id=twin,
            device_id_type=MESH,
        )

    def part_copy(m, e):
        return pltpu.make_async_remote_copy(
            src_ref=keep.at[m, e],
            dst_ref=part.at[m, e],
            send_sem=part_send.at[m, e],
            recv_sem=part_recv.at[m, e],
            device_id=member(m, mine_steps[e], -1),
            device_id_type=MESH,
        )

    def sketch(m, first, count):
        for i in range(first, min(first + count, COLS - 1)):
            delta_copy(m, i).wait_recv()
        block = held[m, first : first + count].reshape(count * ROWS, WIDE)
        return dot_nn(block, omega_pad[m]).reshape(count, ROWS, R)

    def near_step(m, carry):
        keep[m, 0:6] = sketch(m, 0, 6)
        return carry

    def far_step(m, carry):
        odd[m, 0:6] = sketch(m, 6, 6)
        odd_copy(m, 0).start()
        return carry

    def last_step(m, carry):
        got = sketch(m, 12, 4)
        odd[m, 6] = got[2]
        odd[m, 7] = got[1]
        odd_copy(m, 1).start()
        keep[m, 6] = got[0]
        keep[m, 7] = got[3]
        odd_copy(m, 0).wait_recv()
        for e in range(6):
            keep[m, e] = keep[m, e] + pre[m, e]
            part_copy(m, e).start()
        return carry

    def close_step(m, carry):
        odd_copy(m, 1).wait_recv()
        keep[m, 6] = keep[m, 6] + pre[m, 6]
        part_copy(m, 6).start()
        keep[m, 7] = keep[m, 7] + pre[m, 7]
        return carry

    near_step(0, 0)

    @pl.when(at_zero > 0)
    def _():
        own_omega.wait()

    @pl.when(at_zero == 0)
    def _():
        omega_copy(omega_to).wait_recv()

    near_step(1, 0)
    for step in (far_step, last_step, close_step):
        lax.fori_loop(0, MATS, step, 0)
    pending += [odd_copy(m, g) for m in range(MATS) for g in range(2)]
    pending += [part_copy(m, e) for m in range(MATS) for e in range(7)]

    for m in range(MATS):
        value = keep[m, 7]
        for e in range(7):
            part_copy(m, e).wait_recv()
            value = value + part[m, e]
        rows_all[COLS - 1, m] = value

    def rows_core(e):
        return pltpu.make_async_remote_copy(
            src_ref=rows_all.at[mine_steps[e]],
            dst_ref=rows_all.at[twin_steps[e]],
            send_sem=core_send.at[e],
            recv_sem=core_recv.at[e],
            device_id=twin,
            device_id_type=MESH,
        )

    def rows_copy(m, e):
        return pltpu.make_async_remote_copy(
            src_ref=rows_all.at[COLS - 1, m],
            dst_ref=rows_all.at[mine_steps[e], m],
            send_sem=rows_send.at[m, e],
            recv_sem=rows_recv.at[m, e],
            device_id=member(m, mine_steps[e]),
            device_id_type=MESH,
        )

    rows_core(7).start()
    pending.append(rows_core(7))

    rows_core(7).wait_recv()
    mine = jnp.concatenate([rows_all[15, k], rows_all[13, k]], axis=0)
    gram[...] = dot_tn(mine, mine, HIGH) * (1.0 / D)
    for p in range(16):
        for j in range(4):
            h, at = HEIGHTS[j], STARTS[j]
            top = TILE * j + p * h
            packed[p, at : at + h, :] = gram[top : top + h, TILE * j : TILE * j + TILE]

    def slab_copy(d):
        to = xor(q, d, 4)
        return pltpu.make_async_remote_copy(
            src_ref=packed.at[to],
            dst_ref=slabs.at[d],
            send_sem=slab_send.at[d],
            recv_sem=slab_recv.at[d],
            device_id=plane(to),
            device_id_type=MESH,
        )

    for d in range(1, 16):
        slab_copy(d).start()
    pending += [slab_copy(d) for d in range(1, 16)]
    value = packed[q]
    for d in range(1, 16):
        slab_copy(d).wait_recv()
        value = value + slabs[d]
    total[...] = value

    def x_copy(d):
        return pltpu.make_async_remote_copy(
            src_ref=total,
            dst_ref=across.at[d],
            send_sem=x_send.at[d],
            recv_sem=x_recv.at[d],
            device_id=(r, col_of(z_lo, xor(x, d, 2), k)),
            device_id_type=MESH,
        )

    for d in range(1, 4):
        x_copy(d).start()
    pending += [x_copy(d) for d in range(1, 4)]
    for d in range(1, 4):
        x_copy(d).wait_recv()
    spread[q] = (total[...] + across[1]) + (across[2] + across[3])

    def spread_copy(d):
        return pltpu.make_async_remote_copy(
            src_ref=spread.at[q],
            dst_ref=spread.at[q],
            send_sem=spread_send.at[d],
            recv_sem=spread_recv.at[d],
            device_id=plane(xor(q, d, 4)),
            device_id_type=MESH,
        )

    def spread_arrival(d):
        other = xor(q, d, 4)
        return pltpu.make_async_remote_copy(
            src_ref=spread.at[other],
            dst_ref=spread.at[other],
            send_sem=spread_send.at[d],
            recv_sem=spread_recv.at[d],
            device_id=plane(other),
            device_id_type=MESH,
        )

    for d in range(1, 16):
        spread_copy(d).start()
    pending += [spread_copy(d) for d in range(1, 16)]
    for d in range(1, 16):
        spread_arrival(d).wait_recv()
    for e in range(7):
        for m in range(MATS):
            rows_copy(m, e).start()
    pending += [rows_copy(m, e) for m in range(MATS) for e in range(7)]

    gram[...] = jnp.zeros((R, R), jnp.float32)
    for p in range(16):
        for j in range(4):
            h, at = HEIGHTS[j], STARTS[j]
            top = TILE * j + p * h
            gram[top : top + h, TILE * j : TILE * j + TILE] = spread[p, at : at + h, :]

    low[...] = jnp.zeros((R, R), jnp.float32)
    inv[k] = jnp.zeros((R, R), jnp.float32)
    row_at = lax.broadcasted_iota(jnp.int32, (R, TILE), 0)

    def factor_step(b, carry):
        span = pl.ds(pl.multiple_of(b * TILE, TILE), TILE)
        own = invert_factor(gram[span, span])
        panel = dot_nt(gram[:, span], own, HIGH)
        panel = jnp.where(row_at >= (b + 1) * TILE, panel, 0.0)
        done = dot_nn(low[span, :], inv[k], HIGH)
        inv[k, span, :] = -dot_nn(own, done, HIGH)
        inv[k, span, span] = own
        low[:, span] = panel
        gram[...] = gram[...] - dot_nt(panel, panel, HIGH)

        @pl.when(b == 2)
        def _():
            for e in range(7):
                for m in range(MATS):
                    rows_copy(m, e).wait_recv()
                rows_core(e).start()

        return carry

    lax.fori_loop(0, R // TILE, factor_step, 0)
    pending += [rows_core(e) for e in range(7)]

    inv_copy = pltpu.make_async_remote_copy(
        src_ref=inv.at[k],
        dst_ref=inv.at[k],
        send_sem=inv_send,
        recv_sem=inv_recv,
        device_id=twin,
        device_id_type=MESH,
    )
    inv_arrival = pltpu.make_async_remote_copy(
        src_ref=inv.at[1 - k],
        dst_ref=inv.at[1 - k],
        send_sem=inv_send,
        recv_sem=inv_recv,
        device_id=twin,
        device_id_type=MESH,
    )
    inv_copy.start()
    pending.append(inv_copy)
    for e in range(7):
        rows_core(e).wait_recv()
    inv_arrival.wait_recv()

    def out_copy(m, d):
        to = xor(r, d, 3)
        return pltpu.make_async_remote_copy(
            src_ref=out_part.at[m, to],
            dst_ref=in_part.at[m, r],
            send_sem=out_send.at[m, d],
            recv_sem=out_recv.at[m, r],
            device_id=owner(to) if m else (to, c),
            device_id_type=MESH,
        )

    def out_arrival(m, d):
        return pltpu.make_async_remote_copy(
            src_ref=out_part.at[m, d],
            dst_ref=in_part.at[m, d],
            send_sem=out_send.at[m, 0],
            recv_sem=out_recv.at[m, d],
            device_id=holder(d) if m else (d, c),
            device_id_type=MESH,
        )

    own_out = [
        pltpu.make_async_copy(out_part.at[m, r], in_part.at[m, r], own_out_sem.at[m])
        for m in range(MATS)
    ]

    for m in range(MATS):
        factor, every = inv[m], rows_all[:, m].reshape(COLS * ROWS, R)
        factor_hi, every_hi = factor.astype(jnp.bfloat16), every.astype(jnp.bfloat16)
        factor_lo = (factor - f32(factor_hi)).astype(jnp.bfloat16)
        every_lo = (every - f32(every_hi)).astype(jnp.bfloat16)
        for i in range(R // TILE):
            top, deep = TILE * i, TILE * (i + 1)
            hi, lo = factor_hi[top:deep, :deep], factor_lo[top:deep, :deep]
            basis_t[top:deep, :] = (
                dot_nt(hi, every_hi[:, :deep])
                + (dot_nt(hi, every_lo[:, :deep]) + dot_nt(lo, every_hi[:, :deep]))
            ).astype(jnp.bfloat16)

        def project_step(n, carry):
            span = pl.ds(pl.multiple_of(n * 384, TILE), 384)
            block = held[m, :, :, span].reshape(COLS * ROWS, 384)
            got = dot_nn(basis_t[...], block)
            out_part[m, :, :, span] = got.reshape(8, ROWS, 384).astype(jnp.bfloat16)
            return carry

        lax.fori_loop(0, WIDE // 384, project_step, 0)
        for d in range(1, 8):
            out_copy(m, d).start()
        if m:
            @pl.when(at_zero > 0)
            def _():
                own_out[1].start()

            @pl.when(at_zero == 0)
            def _():
                out_copy(1, 0).start()
        else:
            own_out[0].start()
    pending += [out_copy(m, d) for m in range(MATS) for d in range(1, 8)]

    for m in range(MATS):
        basis_ref[m] = dot_nt(rows_all[COLS - 1, m], inv[m], HIGH)

    for m in range(MATS):
        if m:
            @pl.when(at_zero > 0)
            def _():
                own_out[1].wait()

            @pl.when(at_zero == 0)
            def _():
                out_arrival(1, r).wait_recv()
        else:
            own_out[0].wait()
        for d in range(1, 8):
            out_arrival(m, xor(r, d, 3)).wait_recv()
        value = f32(in_part[m, 0])
        for d in range(1, 8):
            value = value + f32(in_part[m, d])
        projected_ref[m] = value[:, :BLOCK] * (1.0 / math.sqrt(D))


    @pl.when(at_zero == 0)
    def _():
        out_copy(1, 0).wait_send()

    finish()


def body(base, adjusted, omega):
    f, b16, sem = jnp.float32, jnp.bfloat16, pltpu.SemaphoreType.DMA
    any_space, vmem = pl.BlockSpec(memory_space=pl.ANY), pl.BlockSpec(memory_space=pltpu.VMEM)
    scratch = [
        pltpu.VMEM((STAGES, MATS, ROWS, WINDOW + TILE), b16),
        pltpu.VMEM((STAGES, MATS, ROWS, WINDOW + TILE), b16),
        pltpu.VMEM((MATS, COLS, ROWS, WIDE), b16),
        pltpu.VMEM((MATS, COLS, ROWS, WIDE), b16),
        pltpu.VMEM((MATS, WIDE, R), b16),
        pltpu.VMEM((MATS, 8, ROWS, R), f),
        pltpu.VMEM((MATS, 8, ROWS, R), f),
        pltpu.VMEM((MATS, 8, ROWS, R), f),
        pltpu.VMEM((MATS, 8, ROWS, R), f),
        pltpu.VMEM((COLS, MATS, ROWS, R), f),
        pltpu.VMEM((R, R), f),
        pltpu.VMEM((16, SLAB, TILE), f),
        pltpu.VMEM((16, SLAB, TILE), f),
        pltpu.VMEM((SLAB, TILE), f),
        pltpu.VMEM((4, SLAB, TILE), f),
        pltpu.VMEM((16, SLAB, TILE), f),
        pltpu.VMEM((R, R), f),
        pltpu.VMEM((MATS, R, R), f),
        pltpu.VMEM((R, COLS * ROWS), b16),
        pltpu.VMEM((MATS, 8, ROWS, WIDE), b16),
        pltpu.VMEM((MATS, 8, ROWS, WIDE), b16),
        sem((2, MATS, STAGES)),
        sem, sem, sem,
        sem((MATS, COLS)), sem((MATS, COLS)),
        sem((MATS, 2)), sem((MATS, 2)),
        sem((MATS, 8)), sem((MATS, 8)),
        sem((MATS, 8)), sem((MATS, 8)),
        sem((8,)), sem((8,)),
        sem((16,)), sem((16,)),
        sem((4,)), sem((4,)),
        sem((16,)), sem((16,)),
        sem, sem,
        sem((MATS, 8)), sem((MATS, 8)), sem((MATS,)),
    ]
    return pl.pallas_call(
        kernel,
        out_shape=(
            jax.ShapeDtypeStruct((MATS, ROWS, R), f),
            jax.ShapeDtypeStruct((MATS, ROWS, BLOCK), f),
        ),
        in_specs=[any_space, any_space, vmem],
        out_specs=(vmem, vmem),
        scratch_shapes=scratch,
        compiler_params=pltpu.CompilerParams(
            collective_id=0, has_side_effects=True, vmem_limit_bytes=62 << 20
        ),
        cost_estimate=pl.CostEstimate(
            flops=10_000_000_000, bytes_accessed=20_000_000, transcendentals=0
        ),
        name="sketch_project",
    )(base, adjusted, omega)


def solution(mesh):
    placed = (P(None, ("row", "col"), None), P(None, ("row", "col"), None), P("col", None))
    return jax.shard_map(
        body,
        mesh=mesh,
        in_specs=placed,
        out_specs=(P(None, ("row", "col"), None), P(None, "row", "col")),
        check_vma=False,
    )
```

```python
import math

import jax
import jax.numpy as jnp
from jax import lax
from jax.experimental import pallas as pl
from jax.experimental.pallas import tpu as pltpu
from jax.sharding import PartitionSpec as P

MESH = pl.DeviceIdType.MESH
HIGH = lax.Precision.HIGHEST
D = 8192
FF = 29568
R = 512
MATS = 2
ROWS = 64
BLOCK = 1848
WIDE = 1920
WINDOW = 2048
STAGES = 4
COLS = 16
TILE = 128
HEIGHTS = (32, 24, 16, 8)
STARTS = (0, 32, 56, 72)
SLAB = 80


def f32(x):
    return x.astype(jnp.float32)


def dot_nt(a, b, precision=None):
    return lax.dot_general(
        a, b, (((1,), (1,)), ((), ())), precision=precision, preferred_element_type=jnp.float32
    )


def dot_tn(a, b, precision=None):
    return lax.dot_general(
        a, b, (((0,), (0,)), ((), ())), precision=precision, preferred_element_type=jnp.float32
    )


def dot_nn(a, b, precision=None):
    return jnp.dot(a, b, precision=precision, preferred_element_type=jnp.float32)


def invert_factor(block):
    count = TILE // 8
    rows = [block[8 * i : 8 * i + 8, :] for i in range(count)]
    shape = (8, TILE)
    lane = lax.broadcasted_iota(jnp.int32, shape, 1)
    sub = lax.broadcasted_iota(jnp.int32, shape, 0)
    for s in range(count):
        cols = {
            (i, j): jnp.broadcast_to(rows[i][:, 8 * s + j : 8 * s + j + 1], shape)
            for i in range(s, count)
            for j in range(8)
        }
        for j in range(8):
            here = lane == 8 * s + j
            pivot = jnp.broadcast_to(cols[s, j][j : j + 1, :], shape)
            inverse = 1.0 / pivot
            row = jnp.where(here, 1.0, jnp.broadcast_to(rows[s][j : j + 1, :], shape))
            heads = {
                j2: jnp.broadcast_to(cols[s, j2][j : j + 1, :], shape) for j2 in range(j + 1, 8)
            }
            for i in range(s, count):
                factor = cols[i, j] * inverse
                clear = here
                if i == s:
                    factor = jnp.where(sub > j, factor, 0.0)
                    clear = here & (sub > j)
                rows[i] = jnp.where(clear, 0.0, rows[i]) - factor * row
                for j2 in range(j + 1, 8):
                    cols[i, j2] = cols[i, j2] - factor * heads[j2]
    out = []
    for i in range(count):
        at = sub + 8 * i
        diagonal = jnp.sum(jnp.where(lane == at, rows[i], 0.0), axis=1, keepdims=True)
        unit = jnp.where(lane < at, rows[i], jnp.where(lane == at, 1.0, 0.0))
        out.append(unit * (1.0 / jnp.sqrt(diagonal)))
    return jnp.concatenate(out, axis=0)


def kernel(
    base_ref, adjusted_ref, omega_ref, basis_ref, projected_ref,
    old, new, source, held, omega_pad, keep, odd, pre, part, rows_all,
    gram, packed, slabs, total, across, spread, low, inv, basis_t, out_part, in_part,
    load_sem, omega_send, omega_recv, own_sem, send_sem, recv_sem, odd_send, odd_recv, part_send, part_recv,
    rows_send, rows_recv, core_send, core_recv, slab_send, slab_recv, x_send, x_recv,
    spread_send, spread_recv, inv_send, inv_recv, out_send, out_recv, own_out_sem,
):
    r, c = lax.axis_index("row"), lax.axis_index("col")
    y, z_hi = r // 2, r % 2
    z_lo, x, k = c // 8, (c // 2) % 4, c % 2
    z = z_hi * 2 + z_lo
    q = y * 4 + z

    def col_of(z_lo_, x_, k_):
        return z_lo_ * 8 + x_ * 2 + k_

    def offsets(s):
        t, g, u, near = s % 3, s // 3, (s + 4) % 16, s // 12
        dx = (1 + 2 * t - 3 * (t // 2)) * (1 - near)
        dz = ((g + 1) % 2) * (1 - near) + ((u + 1) % 2) * near
        dk = (1 - g // 2) * (1 - near) + (((u + 1) // 2) % 2) * near
        return dx, dz, dk

    def place(m, s, sign):
        dx, dz, dk = offsets(s)
        y_ = (y + m * sign * dx + 4) % 4
        x_ = (x + (1 - m) * sign * dx + 4) % 4
        z_ = (z + dz * (2 * z_lo - 1) * (2 * m - 1) + 4) % 4
        return x_, y_, z_, (k + dk) % 2

    def device(x_, y_, z_, k_):
        return (y_ * 2 + z_ // 2, col_of(z_ % 2, x_, k_))

    def member(m, s, sign=1):
        return device(*place(m, s, sign))

    def turned(x_, y_, k_):
        return (x_ + y_ + 2 * k_) % 4

    def turned_from(x_, y_, k_):
        return (x_ - y_ - 2 * k_ + 8) % 4

    def block_of(m, s):
        x_, y_, z_, k_ = place(m, s, 1)
        return col_of(z_ % 2, (1 - m) * x_ + m * turned(x_, y_, k_), k_)

    mine_steps = (6, 7, 8, 9, 10, 11, 12, 15)
    twin_steps = (0, 1, 2, 3, 4, 5, 14, 13)

    def plane(q_):
        y_, z_ = q_ // 4, q_ % 4
        return (y_ * 2 + z_ // 2, col_of(z_ % 2, x, k))

    def xor(a, d, bits):
        out = 0
        for bit in range(bits):
            own = (a // (1 << bit)) % 2
            out = out + ((own + (d // (1 << bit)) % 2) % 2) * (1 << bit)
        return out

    twin = (r, col_of(z_lo, x, 1 - k))
    pending = []

    def finish():
        for copy in pending:
            copy.wait_send()

        @pl.when(still == 0)
        def _():
            omega_copy(omega_to).wait_send()

    def window(f):
        first = (BLOCK * f) // TILE
        start = jnp.minimum(first, (FF - WINDOW) // TILE)
        return start, first - start, BLOCK * f - first * TILE

    def loads(i):
        slot, out = i % STAGES, []
        for m in range(MATS):
            start, _, _ = window(block_of(m, i))
            span = pl.ds(pl.multiple_of(start * TILE, TILE), WINDOW)
            for n, (src, dst) in enumerate(((base_ref, old), (adjusted_ref, new))):
                out.append(
                    pltpu.make_async_copy(
                        src.at[m, :, span],
                        dst.at[slot, m, :, pl.ds(0, WINDOW)],
                        load_sem.at[n, m, slot],
                    )
                )
        return out

    for i in range(STAGES):
        for copy in loads(i):
            copy.start()

    barrier = pltpu.get_barrier_semaphore()
    def greet(to):
        pl.semaphore_signal(barrier, inc=1, device_id=to, device_id_type=MESH)

    for i in range(COLS - 1):
        for m in range(MATS):
            greet(member(m, i))
    for d in range(1, COLS):
        greet(plane(xor(q, d, 4)))

    def owner(to):
        return device(turned(x, y, k), to // 2, (to % 2) * 2 + z_lo, k)

    def holder(of):
        y_ = of // 2
        return device(turned_from(x, y_, k), y_, (of % 2) * 2 + z_lo, k)

    still = 1 - ((y + 2 * k) % 4 + 3) // 4
    for d in range(8):
        to = xor(r, d, 3)
        if d == 0:
            @pl.when(still == 0)
            def _():
                greet(owner(to))
                greet(holder(to))
        else:
            greet(owner(to))
            greet(holder(to))

    omega_pad[0, 0:1840, :] = omega_ref[0:1840, :]
    tail = f32(omega_ref[1840:1848, :])
    omega_pad[0, 1840:1856, :] = jnp.concatenate([tail, jnp.zeros_like(tail)], axis=0).astype(
        jnp.bfloat16
    )
    omega_pad[0, 1856:1920, :] = jnp.zeros((64, R), jnp.bfloat16)

    lane = lax.broadcasted_iota(jnp.int32, (ROWS, TILE), 1)

    def shifted(i, put):
        slot = i % STAGES
        for m in range(MATS):
            _, skip, ahead = window(block_of(m, i))
            turn = (TILE - ahead) % TILE
            last = None
            for t in range(16):
                span = pl.ds(pl.multiple_of((t + skip) * TILE, TILE), TILE)
                tile = f32(new[slot, m, :, span]) - f32(old[slot, m, :, span])
                tile = pltpu.roll(tile, turn, 1)
                if t > 0:
                    value = jnp.where(lane < TILE - ahead, last, tile)
                    if t == 15:
                        value = jnp.where(lane < BLOCK - 14 * TILE, value, 0.0)
                    put(m, (t - 1) * TILE, value.astype(jnp.bfloat16))
                last = tile

    pl.semaphore_wait(barrier, 3 * (COLS - 1) + 16 - 2 * still)

    def omega_copy(to):
        return pltpu.make_async_remote_copy(
            src_ref=omega_pad.at[0],
            dst_ref=omega_pad.at[1],
            send_sem=omega_send,
            recv_sem=omega_recv,
            device_id=to,
            device_id_type=MESH,
        )

    omega_to = device(turned_from(x, y, k), y, z, k)
    own_omega = pltpu.make_async_copy(omega_pad.at[0], omega_pad.at[1], own_sem)

    @pl.when(still == 0)
    def _():
        omega_copy(omega_to).start()

    @pl.when(still > 0)
    def _():
        own_omega.start()

    def delta_copy(m, i):
        return pltpu.make_async_remote_copy(
            src_ref=source.at[m, i],
            dst_ref=held.at[m, i],
            send_sem=send_sem.at[m, i],
            recv_sem=recv_sem.at[m, i],
            device_id=member(m, i),
            device_id_type=MESH,
        )

    def send_step(i, carry):
        for copy in loads(i):
            copy.wait()

        def put(m, at, value):
            source[m, i, :, at : at + TILE] = value

        shifted(i, put)

        @pl.when(i + STAGES < COLS)
        def _():
            for copy in loads(i + STAGES):
                copy.start()

        for m in range(MATS):
            delta_copy(m, i).start()
        return carry

    lax.fori_loop(0, COLS - 1, send_step, 0)
    pending += [delta_copy(m, i) for m in range(MATS) for i in range(COLS - 1)]

    def put_own(m, at, value):
        held[m, COLS - 1, :, at : at + TILE] = value

    for copy in loads(COLS - 1):
        copy.wait()
    shifted(COLS - 1, put_own)

    def odd_copy(m, g):
        span = pl.ds(6 * g, 6 - 4 * g)
        return pltpu.make_async_remote_copy(
            src_ref=odd.at[m, span],
            dst_ref=pre.at[m, span],
            send_sem=odd_send.at[m, g],
            recv_sem=odd_recv.at[m, g],
            device_id=twin,
            device_id_type=MESH,
        )

    def part_copy(m, e):
        return pltpu.make_async_remote_copy(
            src_ref=keep.at[m, e],
            dst_ref=part.at[m, e],
            send_sem=part_send.at[m, e],
            recv_sem=part_recv.at[m, e],
            device_id=member(m, mine_steps[e], -1),
            device_id_type=MESH,
        )

    def sketch(m, first, count):
        for i in range(first, min(first + count, COLS - 1)):
            delta_copy(m, i).wait_recv()
        block = held[m, first : first + count].reshape(count * ROWS, WIDE)
        return dot_nn(block, omega_pad[m]).reshape(count, ROWS, R)

    def far_step(m, carry):
        odd[m, 0:6] = sketch(m, 0, 6)
        odd_copy(m, 0).start()
        return carry

    def last_step(m, carry):
        got = sketch(m, 12, 4)
        odd[m, 6] = got[2]
        odd[m, 7] = got[1]
        odd_copy(m, 1).start()
        keep[m, 6] = got[0]
        keep[m, 7] = got[3]
        return carry

    def near_step(m, carry):
        keep[m, 0:6] = sketch(m, 6, 6)
        odd_copy(m, 0).wait_recv()
        for e in range(6):
            keep[m, e] = keep[m, e] + pre[m, e]
            part_copy(m, e).start()
        return carry

    def close_step(m, carry):
        odd_copy(m, 1).wait_recv()
        keep[m, 6] = keep[m, 6] + pre[m, 6]
        part_copy(m, 6).start()
        keep[m, 7] = keep[m, 7] + pre[m, 7]
        return carry

    @pl.when(still > 0)
    def _():
        own_omega.wait()

    @pl.when(still == 0)
    def _():
        omega_copy(omega_to).wait_recv()

    def sketch_step(i, carry):
        for step in (far_step, last_step, close_step, near_step):
            step(1 - i, carry)
        return carry

    lax.fori_loop(0, MATS, sketch_step, 0)
    pending += [odd_copy(m, g) for m in range(MATS) for g in range(2)]
    pending += [part_copy(m, e) for m in range(MATS) for e in range(7)]

    for m in range(MATS):
        value = keep[m, 7]
        for e in range(7):
            part_copy(m, e).wait_recv()
            value = value + part[m, e]
        rows_all[COLS - 1, m] = value

    def rows_core(e):
        return pltpu.make_async_remote_copy(
            src_ref=rows_all.at[mine_steps[e]],
            dst_ref=rows_all.at[twin_steps[e]],
            send_sem=core_send.at[e],
            recv_sem=core_recv.at[e],
            device_id=twin,
            device_id_type=MESH,
        )

    def rows_copy(m, e):
        return pltpu.make_async_remote_copy(
            src_ref=rows_all.at[COLS - 1, m],
            dst_ref=rows_all.at[mine_steps[e], m],
            send_sem=rows_send.at[m, e],
            recv_sem=rows_recv.at[m, e],
            device_id=member(m, mine_steps[e]),
            device_id_type=MESH,
        )

    rows_core(7).start()
    pending.append(rows_core(7))

    rows_core(7).wait_recv()
    mine = jnp.concatenate([rows_all[15, k], rows_all[13, k]], axis=0)
    gram[...] = dot_tn(mine, mine, HIGH) * (1.0 / D)
    for p in range(16):
        for j in range(4):
            h, at = HEIGHTS[j], STARTS[j]
            top = TILE * j + p * h
            packed[p, at : at + h, :] = gram[top : top + h, TILE * j : TILE * j + TILE]

    def slab_copy(d):
        to = xor(q, d, 4)
        return pltpu.make_async_remote_copy(
            src_ref=packed.at[to],
            dst_ref=slabs.at[d],
            send_sem=slab_send.at[d],
            recv_sem=slab_recv.at[d],
            device_id=plane(to),
            device_id_type=MESH,
        )

    for d in range(1, 16):
        slab_copy(d).start()
    pending += [slab_copy(d) for d in range(1, 16)]
    value = packed[q]
    for d in range(1, 16):
        slab_copy(d).wait_recv()
        value = value + slabs[d]
    total[...] = value

    def x_copy(d):
        return pltpu.make_async_remote_copy(
            src_ref=total,
            dst_ref=across.at[d],
            send_sem=x_send.at[d],
            recv_sem=x_recv.at[d],
            device_id=(r, col_of(z_lo, xor(x, d, 2), k)),
            device_id_type=MESH,
        )

    for d in range(1, 4):
        x_copy(d).start()
    pending += [x_copy(d) for d in range(1, 4)]
    for d in range(1, 4):
        x_copy(d).wait_recv()
    spread[q] = (total[...] + across[1]) + (across[2] + across[3])

    def spread_copy(d):
        return pltpu.make_async_remote_copy(
            src_ref=spread.at[q],
            dst_ref=spread.at[q],
            send_sem=spread_send.at[d],
            recv_sem=spread_recv.at[d],
            device_id=plane(xor(q, d, 4)),
            device_id_type=MESH,
        )

    def spread_arrival(d):
        other = xor(q, d, 4)
        return pltpu.make_async_remote_copy(
            src_ref=spread.at[other],
            dst_ref=spread.at[other],
            send_sem=spread_send.at[d],
            recv_sem=spread_recv.at[d],
            device_id=plane(other),
            device_id_type=MESH,
        )

    for d in range(1, 16):
        spread_copy(d).start()
    pending += [spread_copy(d) for d in range(1, 16)]
    for d in range(1, 16):
        spread_arrival(d).wait_recv()
    for e in range(7):
        for m in range(MATS):
            rows_copy(m, e).start()
    pending += [rows_copy(m, e) for m in range(MATS) for e in range(7)]

    gram[...] = jnp.zeros((R, R), jnp.float32)
    for p in range(16):
        for j in range(4):
            h, at = HEIGHTS[j], STARTS[j]
            top = TILE * j + p * h
            gram[top : top + h, TILE * j : TILE * j + TILE] = spread[p, at : at + h, :]

    low[...] = jnp.zeros((R, R), jnp.float32)
    inv[k] = jnp.zeros((R, R), jnp.float32)
    row_at = lax.broadcasted_iota(jnp.int32, (R, TILE), 0)

    def factor_step(b, carry):
        span = pl.ds(pl.multiple_of(b * TILE, TILE), TILE)
        own = invert_factor(gram[span, span])
        panel = dot_nt(gram[:, span], own, HIGH)
        panel = jnp.where(row_at >= (b + 1) * TILE, panel, 0.0)
        done = dot_nn(low[span, :], inv[k], HIGH)
        inv[k, span, :] = -dot_nn(own, done, HIGH)
        inv[k, span, span] = own
        low[:, span] = panel
        gram[...] = gram[...] - dot_nt(panel, panel, HIGH)

        @pl.when(b == 2)
        def _():
            for e in range(7):
                for m in range(MATS):
                    rows_copy(m, e).wait_recv()
                rows_core(e).start()

        return carry

    lax.fori_loop(0, R // TILE, factor_step, 0)
    pending += [rows_core(e) for e in range(7)]

    inv_copy = pltpu.make_async_remote_copy(
        src_ref=inv.at[k],
        dst_ref=inv.at[k],
        send_sem=inv_send,
        recv_sem=inv_recv,
        device_id=twin,
        device_id_type=MESH,
    )
    inv_arrival = pltpu.make_async_remote_copy(
        src_ref=inv.at[1 - k],
        dst_ref=inv.at[1 - k],
        send_sem=inv_send,
        recv_sem=inv_recv,
        device_id=twin,
        device_id_type=MESH,
    )
    inv_copy.start()
    pending.append(inv_copy)
    for e in range(7):
        rows_core(e).wait_recv()
    inv_arrival.wait_recv()

    def out_copy(m, d):
        to = xor(r, d, 3)
        return pltpu.make_async_remote_copy(
            src_ref=out_part.at[m, to],
            dst_ref=in_part.at[m, r],
            send_sem=out_send.at[m, d],
            recv_sem=out_recv.at[m, r],
            device_id=owner(to) if m else (to, c),
            device_id_type=MESH,
        )

    def out_arrival(m, d):
        return pltpu.make_async_remote_copy(
            src_ref=out_part.at[m, d],
            dst_ref=in_part.at[m, d],
            send_sem=out_send.at[m, 0],
            recv_sem=out_recv.at[m, d],
            device_id=holder(d) if m else (d, c),
            device_id_type=MESH,
        )

    own_out = [
        pltpu.make_async_copy(out_part.at[m, r], in_part.at[m, r], own_out_sem.at[m])
        for m in range(MATS)
    ]

    for m in (1, 0):
        factor, every = inv[m], rows_all[:, m].reshape(COLS * ROWS, R)
        factor_hi, every_hi = factor.astype(jnp.bfloat16), every.astype(jnp.bfloat16)
        factor_lo = (factor - f32(factor_hi)).astype(jnp.bfloat16)
        every_lo = (every - f32(every_hi)).astype(jnp.bfloat16)
        for i in range(R // TILE):
            top, deep = TILE * i, TILE * (i + 1)
            hi, lo = factor_hi[top:deep, :deep], factor_lo[top:deep, :deep]
            basis_t[top:deep, :] = (
                dot_nt(hi, every_hi[:, :deep])
                + (dot_nt(hi, every_lo[:, :deep]) + dot_nt(lo, every_hi[:, :deep]))
            ).astype(jnp.bfloat16)

        def project_step(n, carry):
            span = pl.ds(pl.multiple_of(n * 384, TILE), 384)
            block = held[m, :, :, span].reshape(COLS * ROWS, 384)
            got = dot_nn(basis_t[...], block)
            out_part[m, :, :, span] = got.reshape(8, ROWS, 384).astype(jnp.bfloat16)
            return carry

        lax.fori_loop(0, WIDE // 384, project_step, 0)
        for d in range(1, 8):
            out_copy(m, d).start()
        if m:
            @pl.when(still > 0)
            def _():
                own_out[1].start()

            @pl.when(still == 0)
            def _():
                out_copy(1, 0).start()
        else:
            own_out[0].start()
    pending += [out_copy(m, d) for m in range(MATS) for d in range(1, 8)]

    for m in range(MATS):
        basis_ref[m] = dot_nt(rows_all[COLS - 1, m], inv[m], HIGH)

    for m in (1, 0):
        if m:
            @pl.when(still > 0)
            def _():
                own_out[1].wait()

            @pl.when(still == 0)
            def _():
                out_arrival(1, r).wait_recv()
        else:
            own_out[0].wait()
        for d in range(1, 8):
            out_arrival(m, xor(r, d, 3)).wait_recv()
        value = f32(in_part[m, 0])
        for d in range(1, 8):
            value = value + f32(in_part[m, d])
        projected_ref[m] = value[:, :BLOCK] * (1.0 / math.sqrt(D))


    @pl.when(still == 0)
    def _():
        out_copy(1, 0).wait_send()

    finish()


def body(base, adjusted, omega):
    f, b16, sem = jnp.float32, jnp.bfloat16, pltpu.SemaphoreType.DMA
    any_space, vmem = pl.BlockSpec(memory_space=pl.ANY), pl.BlockSpec(memory_space=pltpu.VMEM)
    scratch = [
        pltpu.VMEM((STAGES, MATS, ROWS, WINDOW + TILE), b16),
        pltpu.VMEM((STAGES, MATS, ROWS, WINDOW + TILE), b16),
        pltpu.VMEM((MATS, COLS, ROWS, WIDE), b16),
        pltpu.VMEM((MATS, COLS, ROWS, WIDE), b16),
        pltpu.VMEM((MATS, WIDE, R), b16),
        pltpu.VMEM((MATS, 8, ROWS, R), f),
        pltpu.VMEM((MATS, 8, ROWS, R), f),
        pltpu.VMEM((MATS, 8, ROWS, R), f),
        pltpu.VMEM((MATS, 8, ROWS, R), f),
        pltpu.VMEM((COLS, MATS, ROWS, R), f),
        pltpu.VMEM((R, R), f),
        pltpu.VMEM((16, SLAB, TILE), f),
        pltpu.VMEM((16, SLAB, TILE), f),
        pltpu.VMEM((SLAB, TILE), f),
        pltpu.VMEM((4, SLAB, TILE), f),
        pltpu.VMEM((16, SLAB, TILE), f),
        pltpu.VMEM((R, R), f),
        pltpu.VMEM((MATS, R, R), f),
        pltpu.VMEM((R, COLS * ROWS), b16),
        pltpu.VMEM((MATS, 8, ROWS, WIDE), b16),
        pltpu.VMEM((MATS, 8, ROWS, WIDE), b16),
        sem((2, MATS, STAGES)),
        sem, sem, sem,
        sem((MATS, COLS)), sem((MATS, COLS)),
        sem((MATS, 2)), sem((MATS, 2)),
        sem((MATS, 8)), sem((MATS, 8)),
        sem((MATS, 8)), sem((MATS, 8)),
        sem((8,)), sem((8,)),
        sem((16,)), sem((16,)),
        sem((4,)), sem((4,)),
        sem((16,)), sem((16,)),
        sem, sem,
        sem((MATS, 8)), sem((MATS, 8)), sem((MATS,)),
    ]
    return pl.pallas_call(
        kernel,
        out_shape=(
            jax.ShapeDtypeStruct((MATS, ROWS, R), f),
            jax.ShapeDtypeStruct((MATS, ROWS, BLOCK), f),
        ),
        in_specs=[any_space, any_space, vmem],
        out_specs=(vmem, vmem),
        scratch_shapes=scratch,
        compiler_params=pltpu.CompilerParams(
            collective_id=0, has_side_effects=True, vmem_limit_bytes=62 << 20
        ),
        cost_estimate=pl.CostEstimate(
            flops=10_000_000_000, bytes_accessed=20_000_000, transcendentals=0
        ),
        name="sketch_project",
    )(base, adjusted, omega)


def solution(mesh):
    placed = (P(None, ("row", "col"), None), P(None, ("row", "col"), None), P("col", None))
    return jax.shard_map(
        body,
        mesh=mesh,
        in_specs=placed,
        out_specs=(P(None, ("row", "col"), None), P(None, "row", "col")),
        check_vma=False,
    )
```

```python
import math

import jax
import jax.numpy as jnp
from jax import lax
from jax.experimental import pallas as pl
from jax.experimental.pallas import tpu as pltpu
from jax.sharding import PartitionSpec as P

MESH = pl.DeviceIdType.MESH
HIGH = lax.Precision.HIGHEST
D = 8192
FF = 29568
R = 512
MATS = 2
ROWS = 64
BLOCK = 1848
WIDE = 1920
WINDOW = 2048
STAGES = 4
COLS = 16
TILE = 128
HEIGHTS = (32, 24, 16, 8)
STARTS = (0, 32, 56, 72)
SLAB = 80


def f32(x):
    return x.astype(jnp.float32)


def dot_nt(a, b, precision=None):
    return lax.dot_general(
        a, b, (((1,), (1,)), ((), ())), precision=precision, preferred_element_type=jnp.float32
    )


def dot_tn(a, b, precision=None):
    return lax.dot_general(
        a, b, (((0,), (0,)), ((), ())), precision=precision, preferred_element_type=jnp.float32
    )


def dot_nn(a, b, precision=None):
    return jnp.dot(a, b, precision=precision, preferred_element_type=jnp.float32)


def invert_factor(block):
    count = TILE // 8
    rows = [block[8 * i : 8 * i + 8, :] for i in range(count)]
    shape = (8, TILE)
    lane = lax.broadcasted_iota(jnp.int32, shape, 1)
    sub = lax.broadcasted_iota(jnp.int32, shape, 0)
    for s in range(count):
        cols = {
            (i, j): jnp.broadcast_to(rows[i][:, 8 * s + j : 8 * s + j + 1], shape)
            for i in range(s, count)
            for j in range(8)
        }
        for j in range(8):
            here = lane == 8 * s + j
            pivot = jnp.broadcast_to(cols[s, j][j : j + 1, :], shape)
            inverse = 1.0 / pivot
            row = jnp.where(here, 1.0, jnp.broadcast_to(rows[s][j : j + 1, :], shape))
            heads = {
                j2: jnp.broadcast_to(cols[s, j2][j : j + 1, :], shape) for j2 in range(j + 1, 8)
            }
            for i in range(s, count):
                factor = cols[i, j] * inverse
                clear = here
                if i == s:
                    factor = jnp.where(sub > j, factor, 0.0)
                    clear = here & (sub > j)
                rows[i] = jnp.where(clear, 0.0, rows[i]) - factor * row
                for j2 in range(j + 1, 8):
                    cols[i, j2] = cols[i, j2] - factor * heads[j2]
    out = []
    for i in range(count):
        at = sub + 8 * i
        diagonal = jnp.sum(jnp.where(lane == at, rows[i], 0.0), axis=1, keepdims=True)
        unit = jnp.where(lane < at, rows[i], jnp.where(lane == at, 1.0, 0.0))
        out.append(unit * (1.0 / jnp.sqrt(diagonal)))
    return jnp.concatenate(out, axis=0)


def kernel(
    base_ref, adjusted_ref, omega_ref, basis_ref, projected_ref,
    old, new, source, held, omega_pad, keep, odd, pre, part, rows_all,
    gram, packed, slabs, total, across, spread, low, inv, basis_t, out_part, in_part,
    load_sem, omega_send, omega_recv, own_sem, send_sem, recv_sem, odd_send, odd_recv, part_send, part_recv,
    rows_send, rows_recv, core_send, core_recv, slab_send, slab_recv, x_send, x_recv,
    spread_send, spread_recv, inv_send, inv_recv, out_send, out_recv, own_out_sem,
):
    r, c = lax.axis_index("row"), lax.axis_index("col")
    y, z_hi = r // 2, r % 2
    z_lo, x, k = c // 8, (c // 2) % 4, c % 2
    z = z_hi * 2 + z_lo
    q = y * 4 + z

    def col_of(z_lo_, x_, k_):
        return z_lo_ * 8 + x_ * 2 + k_

    def offsets(s):
        t, g, u, near = s % 3, s // 3, (s + 4) % 16, s // 12
        dx = (1 + 2 * t - 3 * (t // 2)) * (1 - near)
        dz = ((g + 1) % 2) * (1 - near) + ((u + 1) % 2) * near
        dk = (1 - g // 2) * (1 - near) + (((u + 1) // 2) % 2) * near
        return dx, dz, dk

    def place(m, s, sign):
        dx, dz, dk = offsets(s)
        y_ = (y + m * sign * dx + 4) % 4
        x_ = (x + (1 - m) * sign * dx + 4) % 4
        z_ = (z + dz * (2 * z_lo - 1) * (2 * m - 1) + 4) % 4
        return x_, y_, z_, (k + dk) % 2

    def device(x_, y_, z_, k_):
        return (y_ * 2 + z_ // 2, col_of(z_ % 2, x_, k_))

    def member(m, s, sign=1):
        return device(*place(m, s, sign))

    def turned(x_, y_, k_):
        return (x_ + y_ + 2 * k_) % 4

    def turned_from(x_, y_, k_):
        return (x_ - y_ - 2 * k_ + 8) % 4

    def block_of(m, s):
        x_, y_, z_, k_ = place(m, s, 1)
        return col_of(z_ % 2, (1 - m) * x_ + m * turned(x_, y_, k_), k_)

    mine_steps = (6, 7, 8, 9, 10, 11, 12, 15)
    twin_steps = (0, 1, 2, 3, 4, 5, 14, 13)

    def plane(q_):
        y_, z_ = q_ // 4, q_ % 4
        return (y_ * 2 + z_ // 2, col_of(z_ % 2, x, k))

    def xor(a, d, bits):
        out = 0
        for bit in range(bits):
            own = (a // (1 << bit)) % 2
            out = out + ((own + (d // (1 << bit)) % 2) % 2) * (1 << bit)
        return out

    twin = (r, col_of(z_lo, x, 1 - k))
    pending = []

    def finish():
        for copy in pending:
            copy.wait_send()

        @pl.when(still == 0)
        def _():
            omega_copy(omega_to).wait_send()

    def window(f):
        first = (BLOCK * f) // TILE
        start = jnp.minimum(first, (FF - WINDOW) // TILE)
        return start, first - start, BLOCK * f - first * TILE

    def loads(i):
        slot, out = i % STAGES, []
        for m in range(MATS):
            start, _, _ = window(block_of(m, i))
            span = pl.ds(pl.multiple_of(start * TILE, TILE), WINDOW)
            for n, (src, dst) in enumerate(((base_ref, old), (adjusted_ref, new))):
                out.append(
                    pltpu.make_async_copy(
                        src.at[m, :, span],
                        dst.at[slot, m, :, pl.ds(0, WINDOW)],
                        load_sem.at[n, m, slot],
                    )
                )
        return out

    for i in range(STAGES):
        for copy in loads(i):
            copy.start()

    barrier = pltpu.get_barrier_semaphore()
    def greet(to):
        pl.semaphore_signal(barrier, inc=1, device_id=to, device_id_type=MESH)

    for i in range(COLS - 1):
        for m in range(MATS):
            greet(member(m, i))
    for d in range(1, COLS):
        greet(plane(xor(q, d, 4)))

    def owner(to):
        return device(turned(x, y, k), to // 2, (to % 2) * 2 + z_lo, k)

    def holder(of):
        y_ = of // 2
        return device(turned_from(x, y_, k), y_, (of % 2) * 2 + z_lo, k)

    still = 1 - ((y + 2 * k) % 4 + 3) // 4
    for d in range(8):
        to = xor(r, d, 3)
        if d == 0:
            @pl.when(still == 0)
            def _():
                greet(owner(to))
                greet(holder(to))
        else:
            greet(owner(to))
            greet(holder(to))

    omega_pad[0, 0:1840, :] = omega_ref[0:1840, :]
    tail = f32(omega_ref[1840:1848, :])
    omega_pad[0, 1840:1856, :] = jnp.concatenate([tail, jnp.zeros_like(tail)], axis=0).astype(
        jnp.bfloat16
    )
    omega_pad[0, 1856:1920, :] = jnp.zeros((64, R), jnp.bfloat16)

    lane = lax.broadcasted_iota(jnp.int32, (ROWS, TILE), 1)

    def shifted(i, put):
        slot = i % STAGES
        for m in range(MATS):
            _, skip, ahead = window(block_of(m, i))
            turn = (TILE - ahead) % TILE
            last = None
            for t in range(16):
                span = pl.ds(pl.multiple_of((t + skip) * TILE, TILE), TILE)
                tile = f32(new[slot, m, :, span]) - f32(old[slot, m, :, span])
                tile = pltpu.roll(tile, turn, 1)
                if t > 0:
                    value = jnp.where(lane < TILE - ahead, last, tile)
                    if t == 15:
                        value = jnp.where(lane < BLOCK - 14 * TILE, value, 0.0)
                    put(m, (t - 1) * TILE, value.astype(jnp.bfloat16))
                last = tile

    pl.semaphore_wait(barrier, 3 * (COLS - 1) + 16 - 2 * still)

    def omega_copy(to):
        return pltpu.make_async_remote_copy(
            src_ref=omega_pad.at[0],
            dst_ref=omega_pad.at[1],
            send_sem=omega_send,
            recv_sem=omega_recv,
            device_id=to,
            device_id_type=MESH,
        )

    omega_to = device(turned_from(x, y, k), y, z, k)
    own_omega = pltpu.make_async_copy(omega_pad.at[0], omega_pad.at[1], own_sem)

    @pl.when(still == 0)
    def _():
        omega_copy(omega_to).start()

    @pl.when(still > 0)
    def _():
        own_omega.start()

    def delta_copy(m, i):
        return pltpu.make_async_remote_copy(
            src_ref=source.at[m, i],
            dst_ref=held.at[m, i],
            send_sem=send_sem.at[m, i],
            recv_sem=recv_sem.at[m, i],
            device_id=member(m, i),
            device_id_type=MESH,
        )

    def send_step(i, carry):
        for copy in loads(i):
            copy.wait()

        def put(m, at, value):
            source[m, i, :, at : at + TILE] = value

        shifted(i, put)

        @pl.when(i + STAGES < COLS)
        def _():
            for copy in loads(i + STAGES):
                copy.start()

        for m in range(MATS):
            delta_copy(m, i).start()
        return carry

    lax.fori_loop(0, COLS - 1, send_step, 0)
    pending += [delta_copy(m, i) for m in range(MATS) for i in range(COLS - 1)]

    def put_own(m, at, value):
        held[m, COLS - 1, :, at : at + TILE] = value

    for copy in loads(COLS - 1):
        copy.wait()
    shifted(COLS - 1, put_own)

    def odd_copy(m, g):
        span = pl.ds(6 * g, 6 - 4 * g)
        return pltpu.make_async_remote_copy(
            src_ref=odd.at[m, span],
            dst_ref=pre.at[m, span],
            send_sem=odd_send.at[m, g],
            recv_sem=odd_recv.at[m, g],
            device_id=twin,
            device_id_type=MESH,
        )

    def part_copy(m, e):
        return pltpu.make_async_remote_copy(
            src_ref=keep.at[m, e],
            dst_ref=part.at[m, e],
            send_sem=part_send.at[m, e],
            recv_sem=part_recv.at[m, e],
            device_id=member(m, mine_steps[e], -1),
            device_id_type=MESH,
        )

    def sketch(m, first, count):
        for i in range(first, min(first + count, COLS - 1)):
            delta_copy(m, i).wait_recv()
        block = held[m, first : first + count].reshape(count * ROWS, WIDE)
        return dot_nn(block, omega_pad[m]).reshape(count, ROWS, R)

    def far_step(m, carry):
        odd[m, 0:6] = sketch(m, 0, 6)
        odd_copy(m, 0).start()
        return carry

    def last_step(m, carry):
        got = sketch(m, 12, 4)
        odd[m, 6] = got[2]
        odd[m, 7] = got[1]
        odd_copy(m, 1).start()
        keep[m, 6] = got[0]
        keep[m, 7] = got[3]
        return carry

    def near_step(m, carry):
        keep[m, 0:6] = sketch(m, 6, 6)
        odd_copy(m, 0).wait_recv()
        for e in range(6):
            keep[m, e] = keep[m, e] + pre[m, e]
            part_copy(m, e).start()
        return carry

    def close_step(m, carry):
        odd_copy(m, 1).wait_recv()
        keep[m, 6] = keep[m, 6] + pre[m, 6]
        part_copy(m, 6).start()
        keep[m, 7] = keep[m, 7] + pre[m, 7]
        return carry

    @pl.when(still > 0)
    def _():
        own_omega.wait()

    @pl.when(still == 0)
    def _():
        omega_copy(omega_to).wait_recv()

    def sketch_step(i, carry):
        for step in (far_step, last_step, close_step, near_step):
            step(1 - i, carry)
        return carry

    lax.fori_loop(0, MATS, sketch_step, 0)
    pending += [odd_copy(m, g) for m in range(MATS) for g in range(2)]
    pending += [part_copy(m, e) for m in range(MATS) for e in range(7)]

    for m in range(MATS):
        value = keep[m, 7]
        for e in range(7):
            part_copy(m, e).wait_recv()
            value = value + part[m, e]
        rows_all[COLS - 1, m] = value

    def rows_core(e):
        return pltpu.make_async_remote_copy(
            src_ref=rows_all.at[mine_steps[e]],
            dst_ref=rows_all.at[twin_steps[e]],
            send_sem=core_send.at[e],
            recv_sem=core_recv.at[e],
            device_id=twin,
            device_id_type=MESH,
        )

    def rows_copy(m, e):
        return pltpu.make_async_remote_copy(
            src_ref=rows_all.at[COLS - 1, m],
            dst_ref=rows_all.at[mine_steps[e], m],
            send_sem=rows_send.at[m, e],
            recv_sem=rows_recv.at[m, e],
            device_id=member(m, mine_steps[e]),
            device_id_type=MESH,
        )

    rows_core(7).start()
    pending.append(rows_core(7))

    rows_core(7).wait_recv()
    mine = jnp.concatenate([rows_all[15, k], rows_all[13, k]], axis=0)
    gram[...] = dot_tn(mine, mine, HIGH) * (1.0 / D)
    for p in range(16):
        for j in range(4):
            h, at = HEIGHTS[j], STARTS[j]
            top = TILE * j + p * h
            packed[p, at : at + h, :] = gram[top : top + h, TILE * j : TILE * j + TILE]

    def slab_copy(d):
        to = xor(q, d, 4)
        return pltpu.make_async_remote_copy(
            src_ref=packed.at[to],
            dst_ref=slabs.at[d],
            send_sem=slab_send.at[d],
            recv_sem=slab_recv.at[d],
            device_id=plane(to),
            device_id_type=MESH,
        )

    for d in range(1, 16):
        slab_copy(d).start()
    pending += [slab_copy(d) for d in range(1, 16)]
    value = packed[q]
    for d in range(1, 16):
        slab_copy(d).wait_recv()
        value = value + slabs[d]
    total[...] = value

    def x_copy(d):
        return pltpu.make_async_remote_copy(
            src_ref=total,
            dst_ref=across.at[d],
            send_sem=x_send.at[d],
            recv_sem=x_recv.at[d],
            device_id=(r, col_of(z_lo, xor(x, d, 2), k)),
            device_id_type=MESH,
        )

    for d in range(1, 4):
        x_copy(d).start()
    pending += [x_copy(d) for d in range(1, 4)]
    for d in range(1, 4):
        x_copy(d).wait_recv()
    spread[q] = (total[...] + across[1]) + (across[2] + across[3])

    def spread_copy(d):
        return pltpu.make_async_remote_copy(
            src_ref=spread.at[q],
            dst_ref=spread.at[q],
            send_sem=spread_send.at[d],
            recv_sem=spread_recv.at[d],
            device_id=plane(xor(q, d, 4)),
            device_id_type=MESH,
        )

    def spread_arrival(d):
        other = xor(q, d, 4)
        return pltpu.make_async_remote_copy(
            src_ref=spread.at[other],
            dst_ref=spread.at[other],
            send_sem=spread_send.at[d],
            recv_sem=spread_recv.at[d],
            device_id=plane(other),
            device_id_type=MESH,
        )

    for d in range(1, 16):
        spread_copy(d).start()
    pending += [spread_copy(d) for d in range(1, 16)]
    for d in range(1, 16):
        spread_arrival(d).wait_recv()
    for e in range(7):
        for m in range(MATS):
            rows_copy(m, e).start()
    pending += [rows_copy(m, e) for m in range(MATS) for e in range(7)]

    gram[...] = jnp.zeros((R, R), jnp.float32)
    for p in range(16):
        for j in range(4):
            h, at = HEIGHTS[j], STARTS[j]
            top = TILE * j + p * h
            gram[top : top + h, TILE * j : TILE * j + TILE] = spread[p, at : at + h, :]

    inv[k] = jnp.zeros((R, R), jnp.float32)

    def inv_copy(b):
        span = pl.ds(b * TILE, TILE)
        return pltpu.make_async_remote_copy(
            src_ref=inv.at[k, span],
            dst_ref=inv.at[k, span],
            send_sem=inv_send.at[b],
            recv_sem=inv_recv.at[b],
            device_id=twin,
            device_id_type=MESH,
        )

    def inv_arrival(b):
        span = pl.ds(b * TILE, TILE)
        return pltpu.make_async_remote_copy(
            src_ref=inv.at[1 - k, span],
            dst_ref=inv.at[1 - k, span],
            send_sem=inv_send.at[b],
            recv_sem=inv_recv.at[b],
            device_id=twin,
            device_id_type=MESH,
        )

    def factor_step(b, carry):
        span = pl.ds(pl.multiple_of(b * TILE, TILE), TILE)
        own = invert_factor(gram[span, span])
        inv[k, span, span] = own
        for at in range(4):
            top, end = TILE * at, TILE * (at + 1)

            @pl.when(b == at)
            def _():
                if at < 3:
                    panel = dot_nt(gram[end:, top:end], own, HIGH)
                    low[end:, top:end] = panel
                    gram[end:, end:] = gram[end:, end:] - dot_nt(panel, panel, HIGH)
                if at > 0:
                    done = dot_nn(low[top:end, :top], inv[k, :top, :top], HIGH)
                    inv[k, top:end, :top] = -dot_nn(own, done, HIGH)
                inv_copy(at).start()
                if at == 2:
                    for e in range(7):
                        for m in range(MATS):
                            rows_copy(m, e).wait_recv()
                        rows_core(e).start()

        return carry

    lax.fori_loop(0, R // TILE, factor_step, 0)
    pending += [rows_core(e) for e in range(7)]
    pending += [inv_copy(b) for b in range(4)]

    for e in range(7):
        rows_core(e).wait_recv()
    for b in range(4):
        inv_arrival(b).wait_recv()

    def out_copy(m, d):
        to = xor(r, d, 3)
        return pltpu.make_async_remote_copy(
            src_ref=out_part.at[m, to],
            dst_ref=in_part.at[m, r],
            send_sem=out_send.at[m, d],
            recv_sem=out_recv.at[m, r],
            device_id=owner(to) if m else (to, c),
            device_id_type=MESH,
        )

    def out_arrival(m, d):
        return pltpu.make_async_remote_copy(
            src_ref=out_part.at[m, d],
            dst_ref=in_part.at[m, d],
            send_sem=out_send.at[m, 0],
            recv_sem=out_recv.at[m, d],
            device_id=holder(d) if m else (d, c),
            device_id_type=MESH,
        )

    own_out = [
        pltpu.make_async_copy(out_part.at[m, r], in_part.at[m, r], own_out_sem.at[m])
        for m in range(MATS)
    ]

    for m in (1, 0):
        factor, every = inv[m], rows_all[:, m].reshape(COLS * ROWS, R)
        factor_hi, every_hi = factor.astype(jnp.bfloat16), every.astype(jnp.bfloat16)
        factor_lo = (factor - f32(factor_hi)).astype(jnp.bfloat16)
        every_lo = (every - f32(every_hi)).astype(jnp.bfloat16)
        for i in range(R // TILE):
            top, deep = TILE * i, TILE * (i + 1)
            hi, lo = factor_hi[top:deep, :deep], factor_lo[top:deep, :deep]
            basis_t[top:deep, :] = (
                dot_nt(hi, every_hi[:, :deep])
                + (dot_nt(hi, every_lo[:, :deep]) + dot_nt(lo, every_hi[:, :deep]))
            ).astype(jnp.bfloat16)

        def project_step(n, carry):
            span = pl.ds(pl.multiple_of(n * 384, TILE), 384)
            block = held[m, :, :, span].reshape(COLS * ROWS, 384)
            got = dot_nn(basis_t[...], block)
            out_part[m, :, :, span] = got.reshape(8, ROWS, 384).astype(jnp.bfloat16)
            return carry

        lax.fori_loop(0, WIDE // 384, project_step, 0)
        for d in range(1, 8):
            out_copy(m, d).start()
        if m:
            @pl.when(still > 0)
            def _():
                own_out[1].start()

            @pl.when(still == 0)
            def _():
                out_copy(1, 0).start()
        else:
            own_out[0].start()
    pending += [out_copy(m, d) for m in range(MATS) for d in range(1, 8)]

    for m in range(MATS):
        basis_ref[m] = dot_nt(rows_all[COLS - 1, m], inv[m], HIGH)

    for m in (1, 0):
        if m:
            @pl.when(still > 0)
            def _():
                own_out[1].wait()

            @pl.when(still == 0)
            def _():
                out_arrival(1, r).wait_recv()
        else:
            own_out[0].wait()
        for d in range(1, 8):
            out_arrival(m, xor(r, d, 3)).wait_recv()
        value = f32(in_part[m, 0])
        for d in range(1, 8):
            value = value + f32(in_part[m, d])
        projected_ref[m] = value[:, :BLOCK] * (1.0 / math.sqrt(D))


    @pl.when(still == 0)
    def _():
        out_copy(1, 0).wait_send()

    finish()


def body(base, adjusted, omega):
    f, b16, sem = jnp.float32, jnp.bfloat16, pltpu.SemaphoreType.DMA
    any_space, vmem = pl.BlockSpec(memory_space=pl.ANY), pl.BlockSpec(memory_space=pltpu.VMEM)
    scratch = [
        pltpu.VMEM((STAGES, MATS, ROWS, WINDOW + TILE), b16),
        pltpu.VMEM((STAGES, MATS, ROWS, WINDOW + TILE), b16),
        pltpu.VMEM((MATS, COLS, ROWS, WIDE), b16),
        pltpu.VMEM((MATS, COLS, ROWS, WIDE), b16),
        pltpu.VMEM((MATS, WIDE, R), b16),
        pltpu.VMEM((MATS, 8, ROWS, R), f),
        pltpu.VMEM((MATS, 8, ROWS, R), f),
        pltpu.VMEM((MATS, 8, ROWS, R), f),
        pltpu.VMEM((MATS, 8, ROWS, R), f),
        pltpu.VMEM((COLS, MATS, ROWS, R), f),
        pltpu.VMEM((R, R), f),
        pltpu.VMEM((16, SLAB, TILE), f),
        pltpu.VMEM((16, SLAB, TILE), f),
        pltpu.VMEM((SLAB, TILE), f),
        pltpu.VMEM((4, SLAB, TILE), f),
        pltpu.VMEM((16, SLAB, TILE), f),
        pltpu.VMEM((R, R), f),
        pltpu.VMEM((MATS, R, R), f),
        pltpu.VMEM((R, COLS * ROWS), b16),
        pltpu.VMEM((MATS, 8, ROWS, WIDE), b16),
        pltpu.VMEM((MATS, 8, ROWS, WIDE), b16),
        sem((2, MATS, STAGES)),
        sem, sem, sem,
        sem((MATS, COLS)), sem((MATS, COLS)),
        sem((MATS, 2)), sem((MATS, 2)),
        sem((MATS, 8)), sem((MATS, 8)),
        sem((MATS, 8)), sem((MATS, 8)),
        sem((8,)), sem((8,)),
        sem((16,)), sem((16,)),
        sem((4,)), sem((4,)),
        sem((16,)), sem((16,)),
        sem((4,)), sem((4,)),
        sem((MATS, 8)), sem((MATS, 8)), sem((MATS,)),
    ]
    return pl.pallas_call(
        kernel,
        out_shape=(
            jax.ShapeDtypeStruct((MATS, ROWS, R), f),
            jax.ShapeDtypeStruct((MATS, ROWS, BLOCK), f),
        ),
        in_specs=[any_space, any_space, vmem],
        out_specs=(vmem, vmem),
        scratch_shapes=scratch,
        compiler_params=pltpu.CompilerParams(
            collective_id=0, has_side_effects=True, vmem_limit_bytes=62 << 20
        ),
        cost_estimate=pl.CostEstimate(
            flops=10_000_000_000, bytes_accessed=20_000_000, transcendentals=0
        ),
        name="sketch_project",
    )(base, adjusted, omega)


def solution(mesh):
    placed = (P(None, ("row", "col"), None), P(None, ("row", "col"), None), P("col", None))
    return jax.shard_map(
        body,
        mesh=mesh,
        in_specs=placed,
        out_specs=(P(None, ("row", "col"), None), P(None, "row", "col")),
        check_vma=False,
    )
```

```python
import math

import jax
import jax.numpy as jnp
from jax import lax
from jax.experimental import pallas as pl
from jax.experimental.pallas import tpu as pltpu
from jax.sharding import PartitionSpec as P

MESH = pl.DeviceIdType.MESH
HIGH = lax.Precision.HIGHEST
D = 8192
FF = 29568
R = 512
MATS = 2
ROWS = 64
BLOCK = 1848
WIDE = 1920
WINDOW = 2048
STAGES = 4
COLS = 16
TILE = 128
HEIGHTS = (32, 24, 16, 8)
STARTS = (0, 32, 56, 72)
SLAB = 80


def f32(x):
    return x.astype(jnp.float32)


def dot_nt(a, b, precision=None):
    return lax.dot_general(
        a, b, (((1,), (1,)), ((), ())), precision=precision, preferred_element_type=jnp.float32
    )


def dot_tn(a, b, precision=None):
    return lax.dot_general(
        a, b, (((0,), (0,)), ((), ())), precision=precision, preferred_element_type=jnp.float32
    )


def dot_nn(a, b, precision=None):
    return jnp.dot(a, b, precision=precision, preferred_element_type=jnp.float32)


def invert_factor(block):
    count = TILE // 8
    rows = [block[8 * i : 8 * i + 8, :] for i in range(count)]
    shape = (8, TILE)
    lane = lax.broadcasted_iota(jnp.int32, shape, 1)
    sub = lax.broadcasted_iota(jnp.int32, shape, 0)
    for s in range(count):
        cols = {
            (i, j): jnp.broadcast_to(rows[i][:, 8 * s + j : 8 * s + j + 1], shape)
            for i in range(s, count)
            for j in range(8)
        }
        for j in range(8):
            here = lane == 8 * s + j
            pivot = jnp.broadcast_to(cols[s, j][j : j + 1, :], shape)
            inverse = 1.0 / pivot
            row = jnp.where(here, 1.0, jnp.broadcast_to(rows[s][j : j + 1, :], shape))
            heads = {
                j2: jnp.broadcast_to(cols[s, j2][j : j + 1, :], shape) for j2 in range(j + 1, 8)
            }
            for i in range(s, count):
                factor = cols[i, j] * inverse
                clear = here
                if i == s:
                    factor = jnp.where(sub > j, factor, 0.0)
                    clear = here & (sub > j)
                rows[i] = jnp.where(clear, 0.0, rows[i]) - factor * row
                for j2 in range(j + 1, 8):
                    cols[i, j2] = cols[i, j2] - factor * heads[j2]
    out = []
    for i in range(count):
        at = sub + 8 * i
        diagonal = jnp.sum(jnp.where(lane == at, rows[i], 0.0), axis=1, keepdims=True)
        unit = jnp.where(lane < at, rows[i], jnp.where(lane == at, 1.0, 0.0))
        out.append(unit * (1.0 / jnp.sqrt(diagonal)))
    return jnp.concatenate(out, axis=0)


def kernel(
    base_ref, adjusted_ref, omega_ref, basis_ref, projected_ref,
    old, new, source, held, omega_pad, keep, odd, pre, part, rows_all,
    gram, packed, slabs, total, across, spread, low, inv, basis_t, out_part, in_part,
    load_sem, omega_send, omega_recv, own_sem, send_sem, recv_sem, odd_send, odd_recv, part_send, part_recv,
    rows_send, rows_recv, core_send, core_recv, slab_send, slab_recv, x_send, x_recv,
    spread_send, spread_recv, inv_send, inv_recv, out_send, out_recv, own_out_sem,
):
    r, c = lax.axis_index("row"), lax.axis_index("col")
    y, z_hi = r // 2, r % 2
    z_lo, x, k = c // 8, (c // 2) % 4, c % 2
    z = z_hi * 2 + z_lo
    q = y * 4 + z

    def col_of(z_lo_, x_, k_):
        return z_lo_ * 8 + x_ * 2 + k_

    def offsets(s):
        t, g, u, near = s % 3, s // 3, (s + 4) % 16, s // 12
        dx = (1 + 2 * t - 3 * (t // 2)) * (1 - near)
        dz = ((g + 1) % 2) * (1 - near) + ((u + 1) % 2) * near
        dk = (1 - g // 2) * (1 - near) + (((u + 1) // 2) % 2) * near
        return dx, dz, dk

    def place(m, s, sign):
        dx, dz, dk = offsets(s)
        y_ = (y + m * sign * dx + 4) % 4
        x_ = (x + (1 - m) * sign * dx + 4) % 4
        z_ = (z + dz * (2 * z_lo - 1) * (2 * m - 1) + 4) % 4
        return x_, y_, z_, (k + dk) % 2

    def device(x_, y_, z_, k_):
        return (y_ * 2 + z_ // 2, col_of(z_ % 2, x_, k_))

    def member(m, s, sign=1):
        return device(*place(m, s, sign))

    def turned(x_, y_, k_):
        return (x_ + y_ + 2 * k_) % 4

    def turned_from(x_, y_, k_):
        return (x_ - y_ - 2 * k_ + 8) % 4

    def block_of(m, s):
        x_, y_, z_, k_ = place(m, s, 1)
        return col_of(z_ % 2, (1 - m) * x_ + m * turned(x_, y_, k_), k_)

    mine_steps = (6, 7, 8, 9, 10, 11, 12, 15)
    twin_steps = (0, 1, 2, 3, 4, 5, 14, 13)

    def plane(q_):
        y_, z_ = q_ // 4, q_ % 4
        return (y_ * 2 + z_ // 2, col_of(z_ % 2, x, k))

    def xor(a, d, bits):
        out = 0
        for bit in range(bits):
            own = (a // (1 << bit)) % 2
            out = out + ((own + (d // (1 << bit)) % 2) % 2) * (1 << bit)
        return out

    twin = (r, col_of(z_lo, x, 1 - k))
    pending = []

    def finish():
        for copy in pending:
            copy.wait_send()

        @pl.when(still == 0)
        def _():
            omega_copy(omega_to).wait_send()

    def window(f):
        first = (BLOCK * f) // TILE
        start = jnp.minimum(first, (FF - WINDOW) // TILE)
        return start, first - start, BLOCK * f - first * TILE

    def loads(i):
        slot, out = i % STAGES, []
        for m in range(MATS):
            start, _, _ = window(block_of(m, i))
            span = pl.ds(pl.multiple_of(start * TILE, TILE), WINDOW)
            for n, (src, dst) in enumerate(((base_ref, old), (adjusted_ref, new))):
                out.append(
                    pltpu.make_async_copy(
                        src.at[m, :, span],
                        dst.at[slot, m, :, pl.ds(0, WINDOW)],
                        load_sem.at[n, m, slot],
                    )
                )
        return out

    for i in range(STAGES):
        for copy in loads(i):
            copy.start()

    barrier = pltpu.get_barrier_semaphore()
    def greet(to):
        pl.semaphore_signal(barrier, inc=1, device_id=to, device_id_type=MESH)

    for i in range(COLS - 1):
        for m in range(MATS):
            greet(member(m, i))
    for d in range(1, COLS):
        greet(plane(xor(q, d, 4)))

    def owner(to):
        return device(turned(x, y, k), to // 2, (to % 2) * 2 + z_lo, k)

    def holder(of):
        y_ = of // 2
        return device(turned_from(x, y_, k), y_, (of % 2) * 2 + z_lo, k)

    still = 1 - ((y + 2 * k) % 4 + 3) // 4
    for d in range(8):
        to = xor(r, d, 3)
        if d == 0:
            @pl.when(still == 0)
            def _():
                greet(owner(to))
                greet(holder(to))
        else:
            greet(owner(to))
            greet(holder(to))

    omega_pad[0, 0:1840, :] = omega_ref[0:1840, :]
    tail = f32(omega_ref[1840:1848, :])
    omega_pad[0, 1840:1856, :] = jnp.concatenate([tail, jnp.zeros_like(tail)], axis=0).astype(
        jnp.bfloat16
    )
    omega_pad[0, 1856:1920, :] = jnp.zeros((64, R), jnp.bfloat16)

    lane = lax.broadcasted_iota(jnp.int32, (ROWS, TILE), 1)

    def shifted(i, put):
        slot = i % STAGES
        for m in range(MATS):
            _, skip, ahead = window(block_of(m, i))
            turn = (TILE - ahead) % TILE
            last = None
            for t in range(16):
                span = pl.ds(pl.multiple_of((t + skip) * TILE, TILE), TILE)
                tile = f32(new[slot, m, :, span]) - f32(old[slot, m, :, span])
                tile = pltpu.roll(tile, turn, 1)
                if t > 0:
                    value = jnp.where(lane < TILE - ahead, last, tile)
                    if t == 15:
                        value = jnp.where(lane < BLOCK - 14 * TILE, value, 0.0)
                    put(m, (t - 1) * TILE, value.astype(jnp.bfloat16))
                last = tile

    pl.semaphore_wait(barrier, 3 * (COLS - 1) + 16 - 2 * still)

    def omega_copy(to):
        return pltpu.make_async_remote_copy(
            src_ref=omega_pad.at[0],
            dst_ref=omega_pad.at[1],
            send_sem=omega_send,
            recv_sem=omega_recv,
            device_id=to,
            device_id_type=MESH,
        )

    omega_to = device(turned_from(x, y, k), y, z, k)
    own_omega = pltpu.make_async_copy(omega_pad.at[0], omega_pad.at[1], own_sem)

    @pl.when(still == 0)
    def _():
        omega_copy(omega_to).start()

    @pl.when(still > 0)
    def _():
        own_omega.start()

    def delta_copy(m, i):
        return pltpu.make_async_remote_copy(
            src_ref=source.at[m, i],
            dst_ref=held.at[m, i],
            send_sem=send_sem.at[m, i],
            recv_sem=recv_sem.at[m, i],
            device_id=member(m, i),
            device_id_type=MESH,
        )

    def send_step(i, carry):
        for copy in loads(i):
            copy.wait()

        def put(m, at, value):
            source[m, i, :, at : at + TILE] = value

        shifted(i, put)

        @pl.when(i + STAGES < COLS)
        def _():
            for copy in loads(i + STAGES):
                copy.start()

        for m in range(MATS):
            delta_copy(m, i).start()
        return carry

    lax.fori_loop(0, COLS - 1, send_step, 0)
    pending += [delta_copy(m, i) for m in range(MATS) for i in range(COLS - 1)]

    def put_own(m, at, value):
        held[m, COLS - 1, :, at : at + TILE] = value

    for copy in loads(COLS - 1):
        copy.wait()
    shifted(COLS - 1, put_own)

    def odd_copy(m, g):
        span = pl.ds(6 * g, 6 - 4 * g)
        return pltpu.make_async_remote_copy(
            src_ref=odd.at[m, span],
            dst_ref=pre.at[m, span],
            send_sem=odd_send.at[m, g],
            recv_sem=odd_recv.at[m, g],
            device_id=twin,
            device_id_type=MESH,
        )

    def part_copy(m, e):
        return pltpu.make_async_remote_copy(
            src_ref=keep.at[m, e],
            dst_ref=part.at[m, e],
            send_sem=part_send.at[m, e],
            recv_sem=part_recv.at[m, e],
            device_id=member(m, mine_steps[e], -1),
            device_id_type=MESH,
        )

    def sketch(m, first, count):
        for i in range(first, min(first + count, COLS - 1)):
            delta_copy(m, i).wait_recv()
        block = held[m, first : first + count].reshape(count * ROWS, WIDE)
        return dot_nn(block, omega_pad[m]).reshape(count, ROWS, R)

    def far_step(m, carry):
        odd[m, 0:6] = sketch(m, 0, 6)
        odd_copy(m, 0).start()
        return carry

    def last_step(m, carry):
        got = sketch(m, 12, 4)
        odd[m, 6] = got[2]
        odd[m, 7] = got[1]
        odd_copy(m, 1).start()
        keep[m, 6] = got[0]
        keep[m, 7] = got[3]
        return carry

    def near_step(m, carry):
        keep[m, 0:6] = sketch(m, 6, 6)
        odd_copy(m, 0).wait_recv()
        for e in range(6):
            keep[m, e] = keep[m, e] + pre[m, e]
            part_copy(m, e).start()
        return carry

    def close_step(m, carry):
        odd_copy(m, 1).wait_recv()
        keep[m, 6] = keep[m, 6] + pre[m, 6]
        part_copy(m, 6).start()
        keep[m, 7] = keep[m, 7] + pre[m, 7]
        return carry

    @pl.when(still > 0)
    def _():
        own_omega.wait()

    @pl.when(still == 0)
    def _():
        omega_copy(omega_to).wait_recv()

    def sketch_step(i, carry):
        for step in (far_step, last_step, close_step, near_step):
            step(1 - i, carry)
        return carry

    lax.fori_loop(0, MATS, sketch_step, 0)
    pending += [odd_copy(m, g) for m in range(MATS) for g in range(2)]
    pending += [part_copy(m, e) for m in range(MATS) for e in range(7)]

    for m in range(MATS):
        value = keep[m, 7]
        for e in range(7):
            part_copy(m, e).wait_recv()
            value = value + part[m, e]
        rows_all[COLS - 1, m] = value

    def rows_core(e):
        return pltpu.make_async_remote_copy(
            src_ref=rows_all.at[mine_steps[e]],
            dst_ref=rows_all.at[twin_steps[e]],
            send_sem=core_send.at[e],
            recv_sem=core_recv.at[e],
            device_id=twin,
            device_id_type=MESH,
        )

    def rows_copy(m, e):
        return pltpu.make_async_remote_copy(
            src_ref=rows_all.at[COLS - 1, m],
            dst_ref=rows_all.at[mine_steps[e], m],
            send_sem=rows_send.at[m, e],
            recv_sem=rows_recv.at[m, e],
            device_id=member(m, mine_steps[e]),
            device_id_type=MESH,
        )

    rows_core(7).start()
    pending.append(rows_core(7))

    rows_core(7).wait_recv()
    mine = jnp.concatenate([rows_all[15, k], rows_all[13, k]], axis=0)
    gram[...] = dot_tn(mine, mine, HIGH) * (1.0 / D)
    for p in range(16):
        for j in range(4):
            h, at = HEIGHTS[j], STARTS[j]
            top = TILE * j + p * h
            packed[p, at : at + h, :] = gram[top : top + h, TILE * j : TILE * j + TILE]

    def slab_copy(d):
        to = xor(q, d, 4)
        return pltpu.make_async_remote_copy(
            src_ref=packed.at[to],
            dst_ref=slabs.at[d],
            send_sem=slab_send.at[d],
            recv_sem=slab_recv.at[d],
            device_id=plane(to),
            device_id_type=MESH,
        )

    for d in range(1, 16):
        slab_copy(d).start()
    pending += [slab_copy(d) for d in range(1, 16)]
    value = packed[q]
    for d in range(1, 16):
        slab_copy(d).wait_recv()
        value = value + slabs[d]
    total[...] = value

    def x_copy(d):
        return pltpu.make_async_remote_copy(
            src_ref=total,
            dst_ref=across.at[d],
            send_sem=x_send.at[d],
            recv_sem=x_recv.at[d],
            device_id=(r, col_of(z_lo, xor(x, d, 2), k)),
            device_id_type=MESH,
        )

    for d in range(1, 4):
        x_copy(d).start()
    pending += [x_copy(d) for d in range(1, 4)]
    for d in range(1, 4):
        x_copy(d).wait_recv()
    spread[q] = (total[...] + across[1]) + (across[2] + across[3])

    def spread_copy(d):
        return pltpu.make_async_remote_copy(
            src_ref=spread.at[q],
            dst_ref=spread.at[q],
            send_sem=spread_send.at[d],
            recv_sem=spread_recv.at[d],
            device_id=plane(xor(q, d, 4)),
            device_id_type=MESH,
        )

    def spread_arrival(d):
        other = xor(q, d, 4)
        return pltpu.make_async_remote_copy(
            src_ref=spread.at[other],
            dst_ref=spread.at[other],
            send_sem=spread_send.at[d],
            recv_sem=spread_recv.at[d],
            device_id=plane(other),
            device_id_type=MESH,
        )

    for d in range(1, 16):
        spread_copy(d).start()
    pending += [spread_copy(d) for d in range(1, 16)]
    for d in range(1, 16):
        spread_arrival(d).wait_recv()
    for e in range(7):
        for m in range(MATS):
            rows_copy(m, e).start()
    pending += [rows_copy(m, e) for m in range(MATS) for e in range(7)]

    gram[...] = jnp.zeros((R, R), jnp.float32)
    for p in range(16):
        for j in range(4):
            h, at = HEIGHTS[j], STARTS[j]
            top = TILE * j + p * h
            gram[top : top + h, TILE * j : TILE * j + TILE] = spread[p, at : at + h, :]

    inv[k] = jnp.zeros((R, R), jnp.float32)

    def inv_copy(b):
        span = pl.ds(b * TILE, TILE)
        return pltpu.make_async_remote_copy(
            src_ref=inv.at[k, span],
            dst_ref=inv.at[k, span],
            send_sem=inv_send.at[b],
            recv_sem=inv_recv.at[b],
            device_id=twin,
            device_id_type=MESH,
        )

    def inv_arrival(b):
        span = pl.ds(b * TILE, TILE)
        return pltpu.make_async_remote_copy(
            src_ref=inv.at[1 - k, span],
            dst_ref=inv.at[1 - k, span],
            send_sem=inv_send.at[b],
            recv_sem=inv_recv.at[b],
            device_id=twin,
            device_id_type=MESH,
        )

    def factor_step(b, carry):
        span = pl.ds(pl.multiple_of(b * TILE, TILE), TILE)
        own = invert_factor(gram[span, span])
        inv[k, span, span] = own
        for at in range(4):
            top, end = TILE * at, TILE * (at + 1)

            @pl.when(b == at)
            def _():
                if at < 3:
                    panel = dot_nt(gram[end:, top:end], own, HIGH)
                    low[end:, top:end] = panel
                    gram[end:, end:] = gram[end:, end:] - dot_nt(panel, panel, HIGH)
                if at > 0:
                    done = dot_nn(low[top:end, :top], inv[k, :top, :top], HIGH)
                    inv[k, top:end, :top] = -dot_nn(own, done, HIGH)
                inv_copy(at).start()
                if at == 2:
                    for e in range(7):
                        for m in range(MATS):
                            rows_copy(m, e).wait_recv()
                        rows_core(e).start()

        return carry

    lax.fori_loop(0, R // TILE, factor_step, 0)
    pending += [rows_core(e) for e in range(7)]
    pending += [inv_copy(b) for b in range(4)]

    for e in range(7):
        rows_core(e).wait_recv()
    for b in range(4):
        inv_arrival(b).wait_recv()

    halves = (pl.ds(0, 1152), pl.ds(1152, 768))

    def out_copy(m, d, h):
        to = xor(r, d, 3)
        return pltpu.make_async_remote_copy(
            src_ref=out_part.at[m, to, :, halves[h]],
            dst_ref=in_part.at[m, r, :, halves[h]],
            send_sem=out_send.at[m, d, h],
            recv_sem=out_recv.at[m, r, h],
            device_id=owner(to) if m else (to, c),
            device_id_type=MESH,
        )

    def out_arrival(m, d, h):
        return pltpu.make_async_remote_copy(
            src_ref=out_part.at[m, d, :, halves[h]],
            dst_ref=in_part.at[m, d, :, halves[h]],
            send_sem=out_send.at[m, 0, h],
            recv_sem=out_recv.at[m, d, h],
            device_id=holder(d) if m else (d, c),
            device_id_type=MESH,
        )

    own_out = [
        pltpu.make_async_copy(out_part.at[m, r], in_part.at[m, r], own_out_sem.at[m])
        for m in range(MATS)
    ]

    for m in (1, 0):
        factor, every = inv[m], rows_all[:, m].reshape(COLS * ROWS, R)
        factor_hi, every_hi = factor.astype(jnp.bfloat16), every.astype(jnp.bfloat16)
        factor_lo = (factor - f32(factor_hi)).astype(jnp.bfloat16)
        every_lo = (every - f32(every_hi)).astype(jnp.bfloat16)
        for i in range(R // TILE):
            top, deep = TILE * i, TILE * (i + 1)
            hi, lo = factor_hi[top:deep, :deep], factor_lo[top:deep, :deep]
            basis_t[top:deep, :] = (
                dot_nt(hi, every_hi[:, :deep])
                + (dot_nt(hi, every_lo[:, :deep]) + dot_nt(lo, every_hi[:, :deep]))
            ).astype(jnp.bfloat16)

        def project_step(n, carry):
            span = pl.ds(pl.multiple_of(n * 384, TILE), 384)
            block = held[m, :, :, span].reshape(COLS * ROWS, 384)
            got = dot_nn(basis_t[...], block)
            out_part[m, :, :, span] = got.reshape(8, ROWS, 384).astype(jnp.bfloat16)
            return carry

        for h, (begin, end) in enumerate(((0, 3), (3, 5))):
            lax.fori_loop(begin, end, project_step, 0)
            for d in range(1, 8):
                out_copy(m, d, h).start()
            if m:
                @pl.when(still == 0)
                def _():
                    out_copy(1, 0, h).start()
        if m:
            @pl.when(still > 0)
            def _():
                own_out[1].start()
        else:
            own_out[0].start()
    pending += [out_copy(m, d, h) for m in range(MATS) for d in range(1, 8) for h in range(2)]

    for m in range(MATS):
        basis_ref[m] = dot_nt(rows_all[COLS - 1, m], inv[m], HIGH)

    for m in (1, 0):
        if m:
            @pl.when(still > 0)
            def _():
                own_out[1].wait()

            @pl.when(still == 0)
            def _():
                for h in range(2):
                    out_arrival(1, r, h).wait_recv()
        else:
            own_out[0].wait()
        for d in range(1, 8):
            for h in range(2):
                out_arrival(m, xor(r, d, 3), h).wait_recv()
        value = f32(in_part[m, 0])
        for d in range(1, 8):
            value = value + f32(in_part[m, d])
        projected_ref[m] = value[:, :BLOCK] * (1.0 / math.sqrt(D))


    @pl.when(still == 0)
    def _():
        for h in range(2):
            out_copy(1, 0, h).wait_send()

    finish()


def body(base, adjusted, omega):
    f, b16, sem = jnp.float32, jnp.bfloat16, pltpu.SemaphoreType.DMA
    any_space, vmem = pl.BlockSpec(memory_space=pl.ANY), pl.BlockSpec(memory_space=pltpu.VMEM)
    scratch = [
        pltpu.VMEM((STAGES, MATS, ROWS, WINDOW + TILE), b16),
        pltpu.VMEM((STAGES, MATS, ROWS, WINDOW + TILE), b16),
        pltpu.VMEM((MATS, COLS, ROWS, WIDE), b16),
        pltpu.VMEM((MATS, COLS, ROWS, WIDE), b16),
        pltpu.VMEM((MATS, WIDE, R), b16),
        pltpu.VMEM((MATS, 8, ROWS, R), f),
        pltpu.VMEM((MATS, 8, ROWS, R), f),
        pltpu.VMEM((MATS, 8, ROWS, R), f),
        pltpu.VMEM((MATS, 8, ROWS, R), f),
        pltpu.VMEM((COLS, MATS, ROWS, R), f),
        pltpu.VMEM((R, R), f),
        pltpu.VMEM((16, SLAB, TILE), f),
        pltpu.VMEM((16, SLAB, TILE), f),
        pltpu.VMEM((SLAB, TILE), f),
        pltpu.VMEM((4, SLAB, TILE), f),
        pltpu.VMEM((16, SLAB, TILE), f),
        pltpu.VMEM((R, R), f),
        pltpu.VMEM((MATS, R, R), f),
        pltpu.VMEM((R, COLS * ROWS), b16),
        pltpu.VMEM((MATS, 8, ROWS, WIDE), b16),
        pltpu.VMEM((MATS, 8, ROWS, WIDE), b16),
        sem((2, MATS, STAGES)),
        sem, sem, sem,
        sem((MATS, COLS)), sem((MATS, COLS)),
        sem((MATS, 2)), sem((MATS, 2)),
        sem((MATS, 8)), sem((MATS, 8)),
        sem((MATS, 8)), sem((MATS, 8)),
        sem((8,)), sem((8,)),
        sem((16,)), sem((16,)),
        sem((4,)), sem((4,)),
        sem((16,)), sem((16,)),
        sem((4,)), sem((4,)),
        sem((MATS, 8, 2)), sem((MATS, 8, 2)), sem((MATS,)),
    ]
    return pl.pallas_call(
        kernel,
        out_shape=(
            jax.ShapeDtypeStruct((MATS, ROWS, R), f),
            jax.ShapeDtypeStruct((MATS, ROWS, BLOCK), f),
        ),
        in_specs=[any_space, any_space, vmem],
        out_specs=(vmem, vmem),
        scratch_shapes=scratch,
        compiler_params=pltpu.CompilerParams(
            collective_id=0, has_side_effects=True, vmem_limit_bytes=62 << 20
        ),
        cost_estimate=pl.CostEstimate(
            flops=10_000_000_000, bytes_accessed=20_000_000, transcendentals=0
        ),
        name="sketch_project",
    )(base, adjusted, omega)


def solution(mesh):
    placed = (P(None, ("row", "col"), None), P(None, ("row", "col"), None), P("col", None))
    return jax.shard_map(
        body,
        mesh=mesh,
        in_specs=placed,
        out_specs=(P(None, ("row", "col"), None), P(None, "row", "col")),
        check_vma=False,
    )
```
